32 devices in a mesh: dp: 8 (over z, x), group: 4 (over y, core).
Axes of the slice: x: 2, y: 2, z: 4, core: 2. Of those that a mesh axis runs over, the one named last changes fastest.
Arguments:
- tokens: bfloat16 [1024, 96, 128], P(('dp', 'group')), may hold values from -6 to 6
- lengths: int32 [1024], P(('dp', 'group')), may hold values from 3 to 90, as said below
- norm_gains: float32 [2, 2, 128], replicated, may hold values from 0.5 to 1.5
- norm_shifts: float32 [2, 2, 128], replicated, may hold values from -1.8 to 1.8
- w_qkv: bfloat16 [2, 128, 384], replicated, may hold values from -0.5 to 0.5
- qv_bias: float32 [2, 2, 128], replicated, may hold values from -1.8 to 1.8
- w_out: bfloat16 [2, 128, 128], replicated, may hold values from -1 to 1
- out_biases: float32 [2, 2, 128], replicated, may hold values from -1.8 to 1.8
- w_up: bfloat16 [2, 128, 512], replicated, may hold values from -0.5 to 0.5
- up_bias: float32 [2, 512], replicated, may hold values from -1.8 to 1.8
- w_down: bfloat16 [2, 512, 128], replicated, may hold values from -0.25 to 0.25
- cotangent: bfloat16 [1024, 96, 128], P(('dp', 'group')), may hold values from -6 to 6
Outputs:
- output: bfloat16 [1024, 96, 128], P(('dp', 'group'))
- grad_tokens: bfloat16 [1024, 96, 128], P(('dp', 'group'))
- grad_gains: float32 [2, 2, 128], replicated
- grad_shifts: float32 [2, 2, 128], replicated
- grad_qkv: float32 [2, 128, 384], replicated
- grad_qv_bias: float32 [2, 2, 128], replicated
- grad_out: float32 [2, 128, 128], replicated
- grad_out_biases: float32 [2, 2, 128], replicated
- grad_up: float32 [2, 128, 512], replicated
- grad_up_bias: float32 [2, 512], replicated
- grad_down: float32 [2, 512, 128], replicated
The draws below stay inside these ranges and needn't reach their ends.
Inputs may be any that keep to these rules, and one draw needn't show every extreme that they name: `lengths`: every length is 3 s for a whole number s of timesteps. With e_b = (b * 30) // 8, a trajectory is in band b when e_b < s <= e_(b+1). Among the trajectories of one group (the 4 devices of one dp index) every band holds exactly 16. On one device, bands b and 7 - b together hold at most 12 trajectories, and that many on some device of every group. Some trajectory of every group has 30 timesteps.
All inputs are finite; a program needn't handle non-finite values.
Results may differ from the reference program's by a relative error of at most 0.014.
Values may be sent and summed in bfloat16 or wider, within the bound.
No kernel may reach another device: no remote copies, remote signals or barrier semaphores. Data moves between devices by JAX's collectives and lax.ppermute only.
A program may use at most 128 MiB of HBM per device.

```python
import jax
import jax.numpy as jnp
from jax import lax

D = 128
FF = 512
HEAD = 16
LAYERS = 2
STEPS = 30
SLOT = 96
TRAJ_DEV = 32
TRAJS = 1024
N_DP = 8
N_GROUP = 4


def draw_lengths(key, part):
    key = jax.random.fold_in(key, 11)
    groups = N_DP
    size = N_GROUP
    half = size // 2
    bands = 2 * size
    base = TRAJ_DEV // bands
    keys = jax.random.split(key, 4)
    perm_bands = jax.vmap(lambda kk: jax.random.permutation(kk, size))(jax.random.split(keys[0], groups))
    perm_source = jax.vmap(lambda kk: jax.random.permutation(kk, size))(jax.random.split(keys[1], groups))
    source_iota = jnp.arange(size)
    band_iota = jnp.arange(bands)
    first_oh = (perm_source[:, :half, None] == source_iota).astype(jnp.int32)
    second_oh = (perm_source[:, half:, None] == source_iota).astype(jnp.int32)
    short_band = perm_bands[:, :half]
    long_band = size + (size - 1 - perm_bands[:, half:])
    short_oh = (short_band[:, :, None] == band_iota).astype(jnp.int32)
    long_oh = (long_band[:, :, None] == band_iota).astype(jnp.int32)
    delta = jnp.einsum('gis,gib->gsb', first_oh, long_oh - short_oh) + jnp.einsum('gis,gib->gsb', second_oh, short_oh - long_oh)
    counts = base + base * delta
    bounds = jnp.cumsum(counts, axis=-1)
    place = jnp.arange(TRAJ_DEV)
    band = jnp.sum(place[None, None, :, None] >= bounds[:, :, None, :], axis=-1)
    edges = jnp.arange(bands + 1) * STEPS // bands
    lower = jnp.take(edges, band) + 1
    spread = jnp.take(edges, band + 1) - jnp.take(edges, band)
    draws = jax.random.randint(keys[2], (groups, size, TRAJ_DEV), 0, 1 << 20)
    steps_n = lower + draws % spread
    is_top = band == bands - 1
    first_top = is_top & (jnp.cumsum(is_top.astype(jnp.int32), axis=-1) == 1)
    steps_n = jnp.where(first_top, STEPS, steps_n)
    order_scores = jax.random.randint(keys[3], (groups, size, TRAJ_DEV), 0, 1 << 16) * TRAJ_DEV + place
    order = jnp.argsort(order_scores, axis=-1)
    steps_n = jnp.take_along_axis(steps_n, order, axis=-1)
    return (3 * steps_n).reshape(TRAJS).astype(jnp.int32)


def block_levels(rng, dims, cuts, low, largest):
    factor_of = 1.0
    for dim, shards_of in cuts:
        steps = jax.random.uniform(jax.random.fold_in(jax.random.fold_in(rng, 6), dim), (shards_of,), jnp.float32, low / len(cuts), largest / len(cuts))
        factor_of = factor_of * jnp.repeat(jnp.exp(steps), dims[dim] // shards_of).reshape((-1,) + (1,) * (len(dims) - 1 - dim))
    return factor_of


def normal_values(own_key, extent, scale, limit, cuts=(), kind=jnp.bfloat16):
    array = jax.random.normal(own_key, extent, jnp.float32) * scale
    if len(cuts) > 0:
        array = block_levels(own_key, extent, cuts, -0.22, 0.18) * array
    return jnp.clip(array, min=-limit, max=limit).astype(kind)


def setup_inputs(seed: int = 0) -> dict:
    splits = jax.random.split(jax.random.key(seed), 13)
    return {
        "tokens": normal_values(splits[0], (TRAJS, SLOT, D), 1.0, 6.0, ((0, 32),)),
        "lengths": draw_lengths(jax.random.fold_in(splits[12], 71), 0),
        "norm_gains": jnp.clip(1.0 + 0.1 * jax.random.normal(splits[2], (LAYERS, 2, D), jnp.float32), 0.5, 1.5),
        "norm_shifts": normal_values(splits[3], (LAYERS, 2, D), 0.3, 1.8, (), jnp.float32),
        "w_qkv": normal_values(splits[4], (LAYERS, D, 3 * D), D ** -0.5, 0.5),
        "qv_bias": normal_values(splits[5], (LAYERS, 2, D), 0.3, 1.8, (), jnp.float32),
        "w_out": normal_values(splits[6], (LAYERS, D, D), (D // 4) ** -0.5, 1.0),
        "out_biases": normal_values(splits[7], (LAYERS, 2, D), 0.3, 1.8, (), jnp.float32),
        "w_up": normal_values(splits[8], (LAYERS, D, FF), D ** -0.5, 0.5),
        "up_bias": normal_values(splits[9], (LAYERS, FF), 0.3, 1.8, (), jnp.float32),
        "w_down": normal_values(splits[10], (LAYERS, FF, D), FF ** -0.5, 0.25),
        "cotangent": normal_values(splits[11], (TRAJS, SLOT, D), 1.0, 6.0, ((0, 32),)),
    }


eps = 1e-05
rtg_factor = 0.5
dead_score = -1e+30
block_trajs = 32

@jax.custom_vjp
def low(v):
    return lax.optimization_barrier(v.astype(jnp.bfloat16)).astype(jnp.float32)

@jax.custom_vjp
def low_back(v):
    return v

def low_keep(v):
    return (low(v), None)

def low_pass(kept, grad):
    return (grad,)

def back_keep(v):
    return (v, None)

def back_low(kept, grad):
    return (low(grad),)
low.defvjp(low_keep, low_pass)
low_back.defvjp(back_keep, back_low)

def normalize(stream):
    centered = stream - lax.optimization_barrier(jnp.mean(stream, -1, keepdims=True))
    return centered * lax.rsqrt(lax.optimization_barrier(jnp.mean(centered * centered, -1, keepdims=True)) + eps)

def project(left, right):
    return jnp.einsum('bsd,de->bse', left, right, precision=lax.Precision.HIGHEST)

def layer_apply(stream, layer, params, allowed):
    norm_gains, norm_shifts, w_qkv, qv_bias, w_out, out_biases, w_up, up_bias, w_down = params
    traj_count, row_count, width = stream.shape
    head_count = width // HEAD
    split_shape = (traj_count, row_count, head_count, HEAD)
    normed = low(normalize(stream) * norm_gains[layer, 0] + norm_shifts[layer, 0])
    joint = project(normed, w_qkv[layer])
    query = low(low_back(joint[..., :width] + qv_bias[layer, 0])).reshape(split_shape)
    keys = low(low_back(joint[..., width:2 * width])).reshape(split_shape)
    values = low(low_back(joint[..., 2 * width:] + qv_bias[layer, 1])).reshape(split_shape)
    scores = low_back(jnp.einsum('bqhd,bkhd->bhqk', query, keys, precision=lax.Precision.HIGHEST) * HEAD ** (-0.5))
    scores = jnp.where(allowed, scores, dead_score)
    top_score = lax.optimization_barrier(jnp.max(scores, -1, keepdims=True))
    expo = jnp.exp(scores - top_score)
    probs = expo / lax.optimization_barrier(jnp.sum(expo, -1, keepdims=True))
    attended = jnp.einsum('bhqk,bkhd->bqhd', low(probs), values, precision=lax.Precision.HIGHEST)
    mixed = low(low_back(attended.reshape(traj_count, row_count, width)))
    middle = stream + low_back(project(mixed, w_out[layer]) + out_biases[layer, 0])
    normed_two = low(normalize(middle) * norm_gains[layer, 1] + norm_shifts[layer, 1])
    hidden = low_back(project(normed_two, w_up[layer]) + up_bias[layer])
    active = low(jax.nn.gelu(hidden))
    return middle + low_back(project(active, w_down[layer]) + out_biases[layer, 1])

def forward(tokens_blk, params, lengths_blk):
    positions = jnp.arange(SLOT)
    live = positions[None, :] < lengths_blk[:, None]
    factor = jnp.where(positions % 3 == 0, rtg_factor, 1.0).astype(jnp.float32)
    allowed = (positions[None, :] <= positions[:, None])[None, None] & live[:, None, None, :]
    stream = tokens_blk * factor[None, :, None]
    for layer in range(LAYERS):
        stream = layer_apply(stream, layer, params, allowed)
    return jnp.where(live[..., None], stream, 0.0)

def reference(tokens, lengths, norm_gains, norm_shifts, w_qkv, qv_bias, w_out, out_biases, w_up, up_bias, w_down, cotangent):
    params = tuple((weight.astype(jnp.float32) for weight in (norm_gains, norm_shifts, w_qkv, qv_bias, w_out, out_biases, w_up, up_bias, w_down)))
    width = tokens.shape[-1]
    block_count = tokens.shape[0] // block_trajs
    tok_blocks = tokens.reshape(block_count, block_trajs, SLOT, width)
    len_blocks = lengths.reshape(block_count, block_trajs)
    cot_blocks = cotangent.reshape(block_count, block_trajs, SLOT, width)
    zeros = tuple((jnp.zeros(weight.shape, jnp.float32) for weight in params))

    def step(totals, pieces):
        tok_blk, len_blk, cot_blk = pieces
        outcome, pullback = jax.vjp(lambda tok, *weights: forward(tok, weights, len_blk), tok_blk.astype(jnp.float32), *params)
        grads = pullback(cot_blk.astype(jnp.float32))
        totals = tuple((total + piece for total, piece in zip(totals, grads[1:])))
        return (totals, (outcome.astype(jnp.bfloat16), grads[0].astype(jnp.bfloat16)))
    totals, (outputs, grad_blocks) = lax.scan(step, zeros, (tok_blocks, len_blocks, cot_blocks))
    return (outputs.reshape(tokens.shape), grad_blocks.reshape(tokens.shape), totals[0], totals[1], totals[2], totals[3], totals[4], totals[5], totals[6], totals[7], totals[8])
```

```python
import functools
import jax
import jax.numpy as jnp
from jax import lax
from jax.sharding import PartitionSpec as P
from jax.experimental import pallas as pl
from jax.experimental.pallas import tpu as pltpu

STEPS = 30
HEAD = 16
LAYERS = 2
BIN = 128
MEMBERS = 3
UNIT_BINS = 2
eps = 1e-05
dead_score = -1e30
LOG2E = 1.4426950408889634
LN2 = 0.6931471805599453
GELU_C = 0.7978845608
GELU_K = 0.044715
bf16 = jnp.bfloat16
f32 = jnp.float32


def dot(a, b):
    return lax.dot_general(a, b, (((1,), (0,)), ((), ())), preferred_element_type=f32)


def dot_nt(a, b):
    return lax.dot_general(a, b, (((1,), (1,)), ((), ())), preferred_element_type=f32)


def plan(lengths, order, count, room, used, mem_traj, mem_off, mem_len, steps_top, nbins_ref):
    trajs = lengths.shape[0]

    def clear(i, c):
        count[i] = 0
        return c

    lax.fori_loop(0, steps_top + 1, clear, 0)

    def tally(t, c):
        s = lengths[t] // 3
        count[s] = count[s] + 1
        return c

    lax.fori_loop(0, trajs, tally, 0)

    def prefix(i, total):
        s = steps_top - i
        n = count[s]
        count[s] = total
        return total + n

    lax.fori_loop(0, steps_top + 1, prefix, 0)

    def rank(t, c):
        s = lengths[t] // 3
        p = count[s]
        order[p] = t
        count[s] = p + 1
        return c

    lax.fori_loop(0, trajs, rank, 0)

    def blank(b):
        room[b] = BIN
        used[b] = 0
        for m in range(MEMBERS):
            mem_traj[b * MEMBERS + m] = 0
            mem_off[b * MEMBERS + m] = BIN
            mem_len[b * MEMBERS + m] = 0

    def put(i, nbins):
        t = order[i]
        length = lengths[t]

        def misfit(b):
            return (b < nbins) & ((room[b] < length) | (used[b] >= MEMBERS))

        b = lax.while_loop(misfit, lambda b: b + 1, 0)

        @pl.when(b == nbins)
        def _():
            blank(b)

        slot = b * MEMBERS + used[b]
        mem_traj[slot] = t
        mem_off[slot] = BIN - room[b]
        mem_len[slot] = length
        used[b] = used[b] + 1
        room[b] = room[b] - length
        return jnp.maximum(nbins, b + 1)

    nbins = lax.fori_loop(0, trajs, put, 0)
    for extra in range(UNIT_BINS - 1):
        blank(nbins + extra)
    nbins_ref[0] = nbins
    return nbins


def norm_parts(x):
    c = x - jnp.mean(x, -1, keepdims=True)
    rstd = lax.rsqrt(jnp.mean(c * c, -1, keepdims=True) + eps)
    return c * rstd, rstd


def norm_back(dy, normed, rstd, gain):
    dg = dy * gain
    return (dg - jnp.mean(dg, -1, keepdims=True) - normed * jnp.mean(dg * normed, -1, keepdims=True)) * rstd


def head_masks(width):
    lane = lax.broadcasted_iota(jnp.int32, (1, width), 1) // HEAD
    return [jnp.where(lane == h, 1.0, 0.0).astype(bf16) for h in range(width // HEAD)]


def row_sum(x):
    return jnp.sum(x, 0, keepdims=True)


def main_kernel(
    lengths, tok, cot, gains, shifts, wqkv, qvb, wout, outb, wup, upb, wdown,
    out, gtok, gsum,
    a_qkv, a_out, a_up, a_down, a_small, e_scr, act_scr, gp_scr,
    order, count, room, used, mem_traj, mem_off, mem_len, nbins_ref,
    *, steps_top,
):
    slot_rows, width = tok.shape[1:]
    hidden = wup.shape[2]
    heads = width // HEAD
    pairs = heads // 2
    unit = BIN * UNIT_BINS
    nbins = plan(lengths, order, count, room, used, mem_traj, mem_off, mem_len, steps_top, nbins_ref)
    units = (nbins + UNIT_BINS - 1) // UNIT_BINS
    for ref in (a_qkv, a_out, a_up, a_down, a_small):
        ref[...] = jnp.zeros_like(ref)

    masks = head_masks(width)
    mask_pairs = [
        jnp.concatenate([jnp.broadcast_to(masks[2 * j], (BIN, width)), jnp.broadcast_to(masks[2 * j + 1], (BIN, width))], 0)
        for j in range(pairs)
    ]

    def pair_rows(x, j):
        return jnp.concatenate([x * masks[2 * j], x * masks[2 * j + 1]], 0)

    def body(u, carry):
        r_iota = lax.broadcasted_iota(jnp.int32, (BIN, slot_rows), 0)
        c_iota = lax.broadcasted_iota(jnp.int32, (BIN, slot_rows), 1)
        q_iota = lax.broadcasted_iota(jnp.int32, (BIN, BIN), 0)
        k_iota = lax.broadcasted_iota(jnp.int32, (BIN, BIN), 1)
        toks, cots, biases = [], [], []
        for b in range(UNIT_BINS):
            x = None
            start = jnp.zeros((BIN, BIN), jnp.int32)
            for m in range(MEMBERS):
                slot = (u * UNIT_BINS + b) * MEMBERS + m
                t, o, n = mem_traj[slot], mem_off[slot], mem_len[slot]
                pick = jnp.where((r_iota - o == c_iota) & (c_iota < n), 1.0, 0.0).astype(bf16)
                both = jnp.concatenate([tok[t], cot[t]], axis=1)
                part = dot(pick, both)
                x = part if x is None else x + part
                start = jnp.where(q_iota >= o + n, o + n, start)
            toks.append(x[:, :width])
            cots.append(x[:, width:])
            biases.append(jnp.where((k_iota <= q_iota) & (k_iota >= start), 0.0, dead_score))
        x = jnp.concatenate(toks, 0)
        g = jnp.concatenate(cots, 0)
        row = lax.broadcasted_iota(jnp.int32, (unit, 1), 0) % BIN
        factor = jnp.where(row % 3 == 0, 0.5, 1.0)
        x = x * factor

        saved = []
        for l in range(LAYERS):
            n1, rstd1 = norm_parts(x)
            h1 = (n1 * gains[l, 0:1, :] + shifts[l, 0:1, :]).astype(bf16)
            joint = dot(h1, wqkv[l])
            q = ((joint[:, :width] + qvb[l, 0:1, :]) * (LOG2E * HEAD ** -0.5)).astype(bf16)
            k = joint[:, width:2 * width].astype(bf16)
            v = (joint[:, 2 * width:] + qvb[l, 1:2, :]).astype(bf16)
            mixed_bins, rl_bins = [], []
            for b in range(UNIT_BINS):
                rows = slice(b * BIN, (b + 1) * BIN)
                qb, kb, vb = q[rows], k[rows], v[rows]
                acc = None
                for j in range(pairs):
                    s = dot_nt(qb, pair_rows(kb, j))
                    es = []
                    for half in range(2):
                        sh = s[:, half * BIN:(half + 1) * BIN] + biases[b]
                        es.append(jnp.exp2(sh - jnp.max(sh, -1, keepdims=True)).astype(bf16))
                    e = jnp.concatenate(es, 1)
                    e_scr[l, rows, 2 * j * BIN:(2 * j + 2) * BIN] = e
                    r = jnp.concatenate([pair_rows(vb, j), mask_pairs[j]], 1)
                    part = dot(e, r)
                    acc = part if acc is None else acc + part
                rl = 1.0 / acc[:, width:]
                mixed_bins.append((acc[:, :width] * rl).astype(bf16))
                rl_bins.append(rl)
            mixed = jnp.concatenate(mixed_bins, 0)
            rl = jnp.concatenate(rl_bins, 0)
            x1 = x + dot(mixed, wout[l]) + outb[l, 0:1, :]
            n2, rstd2 = norm_parts(x1)
            h2 = (n2 * gains[l, 1:2, :] + shifts[l, 1:2, :]).astype(bf16)
            hid = dot(h2, wup[l]) + upb[l:l + 1, :]
            sq = hid * hid
            w = 0.5 * jnp.tanh(hid * (GELU_C + (GELU_C * GELU_K) * sq)) + 0.5
            act = hid * w
            gp = w + (act * (1.0 - w)) * (2 * GELU_C + (6 * GELU_C * GELU_K) * sq)
            act_b = act.astype(bf16)
            act_scr[l] = act_b
            gp_scr[l] = gp.astype(bf16)
            saved.append((n1, rstd1, h1, q, k, v, mixed, rl, n2, rstd2, h2))
            x = x1 + dot(act_b, wdown[l]) + outb[l, 1:2, :]

        out_b = x.astype(bf16)
        for l in reversed(range(LAYERS)):
            n1, rstd1, h1, q, k, v, mixed, rl, n2, rstd2, h2 = saved[l]
            e2 = g.astype(bf16)
            a_down[l] += dot(e2.T, act_scr[l])
            a_small[l, 7:8, :] += row_sum(e2.astype(f32))
            da = dot_nt(e2, wdown[l])
            du = (da * gp_scr[l].astype(f32)).astype(bf16)
            a_up[l] += dot(h2.T, du)
            dus = row_sum(du.astype(f32))
            for c in range(hidden // width):
                a_small[l, 8 + c:9 + c, :] += dus[:, c * width:(c + 1) * width]
            dh2 = dot_nt(du, wup[l])
            a_small[l, 1:2, :] += row_sum(dh2 * n2)
            a_small[l, 3:4, :] += row_sum(dh2)
            g1 = g + norm_back(dh2, n2, rstd2, gains[l, 1:2, :])
            e1 = g1.astype(bf16)
            a_out[l] += dot(mixed.T, e1)
            a_small[l, 6:7, :] += row_sum(e1.astype(f32))
            dm = dot_nt(e1, wout[l])
            dm1 = dm * rl
            dmo = -(dm1 * mixed.astype(f32))
            dm1 = dm1.astype(bf16)
            dmo = dmo.astype(bf16)
            dqkv_bins = []
            for b in range(UNIT_BINS):
                rows = slice(b * BIN, (b + 1) * BIN)
                qb, kb, vb = q[rows], k[rows], v[rows]
                lhs = jnp.concatenate([dm1[rows], dmo[rows]], 1)
                dm_t = dm1[rows].T
                q_t = qb.T
                dq = None
                dv_t, dk_t = [], []
                for j in range(pairs):
                    e = e_scr[l, rows, 2 * j * BIN:(2 * j + 2) * BIN]
                    r = jnp.concatenate([pair_rows(vb, j), mask_pairs[j]], 1)
                    ds = e * dot_nt(lhs, r).astype(bf16)
                    part = dot(ds, pair_rows(kb, j))
                    dq = part if dq is None else dq + part
                    top, mid, low = 2 * j * HEAD, (2 * j + 1) * HEAD, (2 * j + 2) * HEAD
                    pv = dot(dm_t[top:low], e)
                    dv_t += [pv[:HEAD, :BIN], pv[HEAD:, BIN:]]
                    pk = dot(q_t[top:low], ds)
                    dk_t += [pk[:HEAD, :BIN], pk[HEAD:, BIN:]]
                dv = jnp.concatenate(dv_t, 0).T
                dk = jnp.concatenate(dk_t, 0).T * LN2
                dqkv_bins.append(jnp.concatenate([(dq * HEAD ** -0.5).astype(bf16), dk.astype(bf16), dv.astype(bf16)], 1))
            dqkv = jnp.concatenate(dqkv_bins, 0)
            a_qkv[l] += dot(h1.T, dqkv)
            sums = row_sum(dqkv.astype(f32))
            a_small[l, 4:5, :] += sums[:, :width]
            a_small[l, 5:6, :] += sums[:, 2 * width:]
            dh = dot_nt(dqkv, wqkv[l])
            a_small[l, 0:1, :] += row_sum(dh * n1)
            a_small[l, 2:3, :] += row_sum(dh)
            g = g1 + norm_back(dh, n1, rstd1, gains[l, 0:1, :])

        grad_b = (g * factor).astype(bf16)
        s_iota = lax.broadcasted_iota(jnp.int32, (slot_rows, BIN), 0)
        p_iota = lax.broadcasted_iota(jnp.int32, (slot_rows, BIN), 1)
        both = jnp.concatenate([out_b, grad_b], 1)
        for b in range(UNIT_BINS):
            for m in range(MEMBERS):
                slot = (u * UNIT_BINS + b) * MEMBERS + m
                t, o, n = mem_traj[slot], mem_off[slot], mem_len[slot]
                pick = jnp.where((p_iota - o == s_iota) & (s_iota < n), 1.0, 0.0).astype(bf16)
                rows = dot(pick, both[b * BIN:(b + 1) * BIN]).astype(bf16)

                @pl.when(n > 0)
                def _():
                    out[t] = rows[:, :width]
                    gtok[t] = rows[:, width:]
        return carry

    lax.fori_loop(0, units, body, 0)

    per_layer = gsum.shape[0] // LAYERS
    for l in range(LAYERS):
        at = l * per_layer
        for c in range(3):
            gsum[at:at + width, :] = a_qkv[l, :, c * width:(c + 1) * width].astype(gsum.dtype)
            at += width
        gsum[at:at + width, :] = a_out[l].astype(gsum.dtype)
        at += width
        for c in range(hidden // width):
            gsum[at:at + width, :] = a_up[l, :, c * width:(c + 1) * width].astype(gsum.dtype)
            at += width
        for c in range(hidden // width):
            gsum[at:at + width, :] = a_down[l, :, c * width:(c + 1) * width].T.astype(gsum.dtype)
            at += width
        gsum[at:at + 64, :] = a_small[l].astype(gsum.dtype)


def main_call(args, steps_top):
    tokens, lengths, gains, shifts, wqkv, qvb, wout, outb, wup, upb, wdown, cot = args
    trajs, slot_rows, width = tokens.shape
    hidden = wup.shape[2]
    unit = BIN * UNIT_BINS
    bins = trajs + UNIT_BINS
    per_layer = 4 * width + 2 * hidden + 64
    vm = pl.BlockSpec(memory_space=pltpu.VMEM)
    sm = pl.BlockSpec(memory_space=pltpu.SMEM)
    return pl.pallas_call(
        functools.partial(main_kernel, steps_top=steps_top),
        out_shape=(
            jax.ShapeDtypeStruct(tokens.shape, bf16),
            jax.ShapeDtypeStruct(tokens.shape, bf16),
            jax.ShapeDtypeStruct((LAYERS * per_layer, width), bf16),
        ),
        in_specs=[sm] + [vm] * 11,
        out_specs=(vm, vm, vm),
        scratch_shapes=[
            pltpu.VMEM((LAYERS, width, 3 * width), f32),
            pltpu.VMEM((LAYERS, width, width), f32),
            pltpu.VMEM((LAYERS, width, hidden), f32),
            pltpu.VMEM((LAYERS, width, hidden), f32),
            pltpu.VMEM((LAYERS, 64, width), f32),
            pltpu.VMEM((LAYERS, unit, width // HEAD * BIN), bf16),
            pltpu.VMEM((LAYERS, unit, hidden), bf16),
            pltpu.VMEM((LAYERS, unit, hidden), bf16),
            pltpu.SMEM((trajs,), jnp.int32),
            pltpu.SMEM((steps_top + 1,), jnp.int32),
            pltpu.SMEM((bins,), jnp.int32),
            pltpu.SMEM((bins,), jnp.int32),
            pltpu.SMEM((bins * MEMBERS,), jnp.int32),
            pltpu.SMEM((bins * MEMBERS,), jnp.int32),
            pltpu.SMEM((bins * MEMBERS,), jnp.int32),
            pltpu.SMEM((1,), jnp.int32),
        ],
        compiler_params=pltpu.CompilerParams(vmem_limit_bytes=56 * 1024 * 1024),
        name="layers",
    )(lengths, tokens, cot, gains, shifts, wqkv, qvb, wout, outb, wup, upb, wdown)


AXES = ("dp", "group")
SPLIT_BITS = 3


def exchange(x, bit, devices):
    return lax.ppermute(x, AXES, [(i, i ^ bit) for i in range(devices)])


def all_sum(x, mesh_shape):
    devices = mesh_shape["dp"] * mesh_shape["group"]
    index = lax.axis_index("dp") * mesh_shape["group"] + lax.axis_index("group")
    bits = [1 << i for i in range(devices.bit_length() - 1)]
    kept = []
    for bit in bits[:SPLIT_BITS]:
        half = x.shape[0] // 2
        low = (index // bit) % 2 == 0
        mine = jnp.where(low, x[:half], x[half:])
        other = jnp.where(low, x[half:], x[:half])
        x = (mine.astype(f32) + exchange(other, bit, devices).astype(f32)).astype(bf16)
        kept.append((bit, low))
    for bit in bits[SPLIT_BITS:]:
        x = (x.astype(f32) + exchange(x, bit, devices).astype(f32)).astype(bf16)
    for bit, low in reversed(kept):
        other = exchange(x, bit, devices)
        x = jnp.where(low, jnp.concatenate([x, other]), jnp.concatenate([other, x]))
    return x


def solution(mesh):
    mesh_shape = dict(mesh.shape)

    def per_device(*args):
        width = args[0].shape[2]
        hidden = args[8].shape[2]
        output, grad_tokens, sums = main_call(args, STEPS)
        total = all_sum(sums, mesh_shape).astype(f32).reshape(LAYERS, -1, width)

        def wide(first, parts):
            return jnp.concatenate([total[:, first + i * width:first + (i + 1) * width] for i in range(parts)], 2)

        up_at = 4 * width
        down_at = up_at + hidden
        small = total[:, down_at + hidden:]
        return (
            output,
            grad_tokens,
            small[:, 0:2],
            small[:, 2:4],
            wide(0, 3),
            small[:, 4:6],
            total[:, 3 * width:4 * width],
            small[:, 6:8],
            wide(up_at, hidden // width),
            small[:, 8:8 + hidden // width].reshape(LAYERS, hidden),
            total[:, down_at:down_at + hidden],
        )

    rows = P(AXES, None, None)
    return jax.shard_map(
        per_device,
        mesh=mesh,
        in_specs=(rows, P(AXES)) + (P(),) * 9 + (rows,),
        out_specs=(rows, rows) + (P(),) * 9,
        check_vma=False,
    )
```

```python
import functools
import jax
import jax.numpy as jnp
from jax import lax
from jax.sharding import PartitionSpec as P
from jax.experimental import pallas as pl
from jax.experimental.pallas import tpu as pltpu

STEPS = 30
HEAD = 16
LAYERS = 2
BIN = 128
SMALL = 64
MEMBERS = 2
UNIT_BINS = 8
eps = 1e-05
dead_score = -1e30
LOG2E = 1.4426950408889634
LN2 = 0.6931471805599453
GELU_C = 0.7978845608
GELU_K = 0.044715
bf16 = jnp.bfloat16
f32 = jnp.float32


def dot(a, b):
    return lax.dot_general(a, b, (((1,), (0,)), ((), ())), preferred_element_type=f32)


def dot_nt(a, b):
    return lax.dot_general(a, b, (((1,), (1,)), ((), ())), preferred_element_type=f32)


def plan(lengths, order, count, mem_traj, mem_off, mem_len, steps_top):
    trajs = lengths.shape[0]
    pairs = trajs // 2

    def clear(i, c):
        count[i] = 0
        return c

    lax.fori_loop(0, steps_top + 1, clear, 0, unroll=True)

    def tally(t, c):
        s = lengths[t] // 3
        count[s] = count[s] + 1
        return c

    lax.fori_loop(0, trajs, tally, 0, unroll=4)

    def prefix(i, total):
        s = steps_top - i
        n = count[s]
        count[s] = total
        return total + n

    lax.fori_loop(0, steps_top + 1, prefix, 0, unroll=True)

    def rank(t, c):
        s = lengths[t] // 3
        p = count[s]
        order[p] = t
        count[s] = p + 1
        return c

    lax.fori_loop(0, trajs, rank, 0, unroll=4)

    def member(slot, t, offset, length):
        mem_traj[slot] = t
        mem_off[slot] = offset
        mem_len[slot] = length

    def pair(p, nbins):
        long, short = order[p], order[trajs - 1 - p]
        length, length_two = lengths[long], lengths[short]
        fits = length + length_two <= BIN
        member(2 * p, long, 0, length)
        member(2 * p + 1, short, length, jnp.where(fits, length_two, 0))
        member(2 * nbins, short, 0, length_two)
        member(2 * nbins + 1, short, length_two, 0)
        return nbins + jnp.where(fits, 0, 1)

    nbins = lax.fori_loop(0, pairs, pair, pairs)
    units = (nbins + UNIT_BINS - 1) // UNIT_BINS

    def pad(i, c):
        member(i, 0, BIN, 0)
        return c

    lax.fori_loop(2 * nbins, 2 * UNIT_BINS * units, pad, 0)
    return units


def norm_parts(x):
    c = x - jnp.mean(x, -1, keepdims=True)
    rstd = lax.rsqrt(jnp.mean(c * c, -1, keepdims=True) + eps)
    return c * rstd, rstd


def norm_back(dy, normed, rstd, gain):
    dg = dy * gain
    return (dg - jnp.mean(dg, -1, keepdims=True) - normed * jnp.mean(dg * normed, -1, keepdims=True)) * rstd


def head_masks(width):
    lane = lax.broadcasted_iota(jnp.int32, (1, width), 1) // HEAD
    return [jnp.where(lane == h, 1.0, 0.0).astype(bf16) for h in range(width // HEAD)]


def row_sum(x):
    return jnp.sum(x, 0, keepdims=True)


def main_kernel(
    lengths, parity, tok_hbm, cot_hbm, gains, shifts, wqkv, qvb, wout, outb, wup, upb, wdown,
    out_hbm, gtok_hbm, mine_hbm, other_hbm,
    tok, cot, out, gtok, gsum,
    a_qkv, a_out, a_up, a_down, a_small, e_scr, act_scr, gp_scr,
    order, count, mem_traj, mem_off, mem_len, sems,
    *, steps_top,
):
    trajs, slot_rows, width = tok.shape
    hidden = wup.shape[2]
    heads = width // HEAD
    pairs = heads // 2
    unit = BIN * UNIT_BINS
    loads = [pltpu.make_async_copy(tok_hbm, tok, sems.at[0]), pltpu.make_async_copy(cot_hbm, cot, sems.at[1])]
    for copy in loads:
        copy.start()
    for ref in (a_qkv, a_out, a_up, a_down, a_small):
        ref[...] = jnp.zeros_like(ref)
    units = plan(lengths, order, count, mem_traj, mem_off, mem_len, steps_top)
    for copy in loads:
        copy.wait()

    masks = head_masks(width)
    mask_pairs = [
        jnp.concatenate([jnp.broadcast_to(masks[2 * j], (BIN, width)), jnp.broadcast_to(masks[2 * j + 1], (BIN, width))], 0)
        for j in range(pairs)
    ]

    def pair_rows(x, j):
        return jnp.concatenate([x * masks[2 * j], x * masks[2 * j + 1]], 0)

    blank = jnp.zeros((HEAD, BIN), bf16)
    ones = jnp.ones((HEAD, BIN), bf16)

    def pair_columns(xt, j):
        lo, mid, hi = 2 * j * HEAD, (2 * j + 1) * HEAD, (2 * j + 2) * HEAD
        parts = [
            jnp.concatenate([xt[lo:mid], blank], 1),
            jnp.concatenate([blank, xt[mid:hi]], 1),
        ]
        if j > 0:
            parts = [jnp.zeros((lo, 2 * BIN), bf16)] + parts
        if hi < width:
            parts = parts + [jnp.zeros((width - hi, 2 * BIN), bf16)]
        return jnp.concatenate(parts, 0)

    ones_t = jnp.ones((width, BIN), bf16)
    mask_columns = [pair_columns(ones_t, j) for j in range(pairs)]

    def body(u, carry):
        r_iota = lax.broadcasted_iota(jnp.int32, (BIN, slot_rows), 0)
        c_iota = lax.broadcasted_iota(jnp.int32, (BIN, slot_rows), 1)
        q_iota = lax.broadcasted_iota(jnp.int32, (BIN, BIN), 0)
        k_iota = lax.broadcasted_iota(jnp.int32, (BIN, BIN), 1)
        toks, cots, biases = [], [], []
        for b in range(UNIT_BINS):
            x = None
            start = jnp.zeros((BIN, BIN), jnp.int32)
            for m in range(MEMBERS):
                slot = (u * UNIT_BINS + b) * MEMBERS + m
                t, o, n = mem_traj[slot], mem_off[slot], mem_len[slot]
                pick = jnp.where((r_iota - o == c_iota) & (c_iota < n), 1.0, 0.0).astype(bf16)
                both = jnp.concatenate([tok[t], cot[t]], axis=1)
                part = dot(pick, both)
                x = part if x is None else x + part
                start = jnp.where(q_iota >= o + n, o + n, start)
            toks.append(x[:, :width])
            cots.append(x[:, width:])
            biases.append(jnp.where((k_iota <= q_iota) & (k_iota >= start), 0.0, dead_score))
        x = jnp.concatenate(toks, 0)
        g = jnp.concatenate(cots, 0)
        row = lax.broadcasted_iota(jnp.int32, (unit, 1), 0) % BIN
        factor = jnp.where(row % 3 == 0, 0.5, 1.0)
        x = x * factor

        saved = []
        for l in range(LAYERS):
            n1, rstd1 = norm_parts(x)
            h1 = (n1 * gains[l, 0:1, :] + shifts[l, 0:1, :]).astype(bf16)
            joint = dot(h1, wqkv[l])
            q = ((joint[:, :width] + qvb[l, 0:1, :]) * (LOG2E * HEAD ** -0.5)).astype(bf16)
            k = joint[:, width:2 * width].astype(bf16)
            v = (joint[:, 2 * width:] + qvb[l, 1:2, :]).astype(bf16)
            bins = range(UNIT_BINS)
            rows_of = [slice(b * BIN, (b + 1) * BIN) for b in bins]
            acc = [None] * UNIT_BINS

            def scores(j):
                return [dot_nt(q[rows_of[b]], pair_rows(k[rows_of[b]], j)) for b in bins]

            ahead = scores(0)
            for j in range(pairs):
                s = ahead
                if j + 1 < pairs:
                    ahead = scores(j + 1)
                es = []
                for b in bins:
                    halves = []
                    for half in range(2):
                        sh = s[b][:, half * BIN:(half + 1) * BIN] + biases[b]
                        halves.append(jnp.exp2(sh - jnp.max(sh, -1, keepdims=True)).astype(bf16))
                    e = jnp.concatenate(halves, 1)
                    e_scr[l, rows_of[b], 2 * j * BIN:(2 * j + 2) * BIN] = e
                    es.append(e)
                for b in bins:
                    r = jnp.concatenate([pair_rows(v[rows_of[b]], j), mask_pairs[j]], 1)
                    part = dot(es[b], r)
                    acc[b] = part if acc[b] is None else acc[b] + part
            mixed_bins, rl_bins = [], []
            for b in bins:
                rl = 1.0 / acc[b][:, width:]
                mixed_bins.append((acc[b][:, :width] * rl).astype(bf16))
                rl_bins.append(rl)
            mixed = jnp.concatenate(mixed_bins, 0)
            rl = jnp.concatenate(rl_bins, 0)
            x1 = x + dot(mixed, wout[l]) + outb[l, 0:1, :]
            n2, rstd2 = norm_parts(x1)
            h2 = (n2 * gains[l, 1:2, :] + shifts[l, 1:2, :]).astype(bf16)
            hid = dot(h2, wup[l]) + upb[l:l + 1, :]
            sq = hid * hid
            w = 0.5 * jnp.tanh(hid * (GELU_C + (GELU_C * GELU_K) * sq)) + 0.5
            act = hid * w
            gp = w + (act * (1.0 - w)) * (2 * GELU_C + (6 * GELU_C * GELU_K) * sq)
            act_b = act.astype(bf16)
            act_scr[l] = act_b
            gp_scr[l] = gp.astype(bf16)
            saved.append((n1, rstd1, h1, q, k, v, mixed, rl, n2, rstd2, h2))
            x = x1 + dot(act_b, wdown[l]) + outb[l, 1:2, :]

        out_b = x.astype(bf16)
        for l in reversed(range(LAYERS)):
            n1, rstd1, h1, q, k, v, mixed, rl, n2, rstd2, h2 = saved[l]
            e2 = g.astype(bf16)
            a_down[l] += dot(e2.T, act_scr[l])
            a_small[l, 7:8, :] += row_sum(e2.astype(f32))
            da = dot_nt(e2, wdown[l])
            du = (da * gp_scr[l].astype(f32)).astype(bf16)
            a_up[l] += dot(h2.T, du)
            dus = row_sum(du.astype(f32))
            for c in range(hidden // width):
                a_small[l, 8 + c:9 + c, :] += dus[:, c * width:(c + 1) * width]
            dh2 = dot_nt(du, wup[l])
            a_small[l, 1:2, :] += row_sum(dh2 * n2)
            a_small[l, 3:4, :] += row_sum(dh2)
            g1 = g + norm_back(dh2, n2, rstd2, gains[l, 1:2, :])
            e1 = g1.astype(bf16)
            a_out[l] += dot(mixed.T, e1)
            a_small[l, 6:7, :] += row_sum(e1.astype(f32))
            dm = dot_nt(e1, wout[l])
            dm1 = dm * rl
            dmo = -(dm1 * mixed.astype(f32))
            dm1 = dm1.astype(bf16)
            dmo = dmo.astype(bf16)
            lhs, dm_t, q_t, v_t, dq, dv_t, dk_t = [], [], [], [], [], [], []
            for b in range(UNIT_BINS):
                rows = slice(b * BIN, (b + 1) * BIN)
                lhs.append(jnp.concatenate([dm1[rows], dmo[rows]], 1))
                dm_t.append(dm1[rows].T)
                q_t.append(q[rows].T)
                v_t.append(v[rows].T)
                dq.append(None)
                dv_t.append([])
                dk_t.append([])
            bins = range(UNIT_BINS)
            rows_of = [slice(b * BIN, (b + 1) * BIN) for b in bins]

            def d_scores(j):
                return [dot(lhs[b], jnp.concatenate([pair_columns(v_t[b], j), mask_columns[j]], 0)) for b in bins]

            ahead = d_scores(0)
            for j in range(pairs):
                top, low = 2 * j * HEAD, (2 * j + 2) * HEAD
                z = ahead
                if j + 1 < pairs:
                    ahead = d_scores(j + 1)
                es = [e_scr[l, rows_of[b], 2 * j * BIN:(2 * j + 2) * BIN] for b in bins]
                for b in bins:
                    pv = dot(dm_t[b][top:low], es[b])
                    dv_t[b] += [pv[:HEAD, :BIN], pv[HEAD:, BIN:]]
                ds = [es[b] * z[b].astype(bf16) for b in bins]
                for b in bins:
                    part = dot(ds[b], pair_rows(k[rows_of[b]], j))
                    dq[b] = part if dq[b] is None else dq[b] + part
                for b in bins:
                    pk = dot(q_t[b][top:low], ds[b])
                    dk_t[b] += [pk[:HEAD, :BIN], pk[HEAD:, BIN:]]
            dqkv_bins = []
            for b in range(UNIT_BINS):
                dv = jnp.concatenate(dv_t[b], 0).T
                dk = jnp.concatenate(dk_t[b], 0).T * LN2
                dqkv_bins.append(jnp.concatenate([(dq[b] * HEAD ** -0.5).astype(bf16), dk.astype(bf16), dv.astype(bf16)], 1))
            dqkv = jnp.concatenate(dqkv_bins, 0)
            a_qkv[l] += dot(h1.T, dqkv)
            sums = row_sum(dqkv.astype(f32))
            a_small[l, 4:5, :] += sums[:, :width]
            a_small[l, 5:6, :] += sums[:, 2 * width:]
            dh = dot_nt(dqkv, wqkv[l])
            a_small[l, 0:1, :] += row_sum(dh * n1)
            a_small[l, 2:3, :] += row_sum(dh)
            g = g1 + norm_back(dh, n1, rstd1, gains[l, 0:1, :])

        grad_b = (g * factor).astype(bf16)
        s_iota = lax.broadcasted_iota(jnp.int32, (slot_rows, BIN), 0)
        p_iota = lax.broadcasted_iota(jnp.int32, (slot_rows, BIN), 1)
        both = jnp.concatenate([out_b, grad_b], 1)
        for b in range(UNIT_BINS):
            for m in range(MEMBERS):
                slot = (u * UNIT_BINS + b) * MEMBERS + m
                t, o, n = mem_traj[slot], mem_off[slot], mem_len[slot]
                pick = jnp.where((p_iota - o == s_iota) & (s_iota < n), 1.0, 0.0).astype(bf16)
                rows = dot(pick, both[b * BIN:(b + 1) * BIN]).astype(bf16)

                home = jnp.where(n > 0, t, trajs)
                out[home] = rows[:, :width]
                gtok[home] = rows[:, width:]
        return carry

    lax.fori_loop(0, units, body, 0)

    stores = [
        pltpu.make_async_copy(out.at[pl.ds(0, trajs)], out_hbm, sems.at[0]),
        pltpu.make_async_copy(gtok.at[pl.ds(0, trajs)], gtok_hbm, sems.at[1]),
    ]
    for copy in stores:
        copy.start()
    for l in range(LAYERS):
        at = 0
        for c in range(3):
            gsum[l, at:at + width, :] = a_qkv[l, :, c * width:(c + 1) * width].astype(bf16)
            at += width
        gsum[l, at:at + width, :] = a_out[l].astype(bf16)
        at += width
        for c in range(hidden // width):
            gsum[l, at:at + width, :] = a_up[l, :, c * width:(c + 1) * width].astype(bf16)
            at += width
        for c in range(hidden // width):
            gsum[l, at:at + width, :] = a_down[l, :, c * width:(c + 1) * width].T.astype(bf16)
            at += width
        gsum[l, at:at + SMALL, :] = a_small[l].astype(bf16)
    mine = parity[0]
    stores += [
        pltpu.make_async_copy(gsum.at[mine], mine_hbm, sems.at[2]),
        pltpu.make_async_copy(gsum.at[1 - mine], other_hbm, sems.at[3]),
    ]
    for copy in stores[2:]:
        copy.start()
    for copy in stores:
        copy.wait()


def main_call(args, steps_top, parity):
    tokens, lengths, gains, shifts, wqkv, qvb, wout, outb, wup, upb, wdown, cot = args
    trajs, slot_rows, width = tokens.shape
    hidden = wup.shape[2]
    unit = BIN * UNIT_BINS
    slots = 2 * (trajs + UNIT_BINS)
    per_layer = 4 * width + 2 * hidden + SMALL
    vm = pl.BlockSpec(memory_space=pltpu.VMEM)
    sm = pl.BlockSpec(memory_space=pltpu.SMEM)
    hbm = pl.BlockSpec(memory_space=pl.ANY)
    sums = jax.ShapeDtypeStruct((per_layer, width), bf16)
    return pl.pallas_call(
        functools.partial(main_kernel, steps_top=steps_top),
        out_shape=(
            jax.ShapeDtypeStruct(tokens.shape, bf16),
            jax.ShapeDtypeStruct(tokens.shape, bf16),
            sums,
            sums,
        ),
        in_specs=[sm, sm, hbm, hbm] + [vm] * 9,
        out_specs=(hbm, hbm, hbm, hbm),
        scratch_shapes=[
            pltpu.VMEM(tokens.shape, bf16),
            pltpu.VMEM(tokens.shape, bf16),
            pltpu.VMEM((trajs + 1, slot_rows, width), bf16),
            pltpu.VMEM((trajs + 1, slot_rows, width), bf16),
            pltpu.VMEM((LAYERS, per_layer, width), bf16),
            pltpu.VMEM((LAYERS, width, 3 * width), f32),
            pltpu.VMEM((LAYERS, width, width), f32),
            pltpu.VMEM((LAYERS, width, hidden), f32),
            pltpu.VMEM((LAYERS, width, hidden), f32),
            pltpu.VMEM((LAYERS, SMALL, width), f32),
            pltpu.VMEM((LAYERS, unit, width // HEAD * BIN), bf16),
            pltpu.VMEM((LAYERS, unit, hidden), bf16),
            pltpu.VMEM((LAYERS, unit, hidden), bf16),
            pltpu.SMEM((trajs,), jnp.int32),
            pltpu.SMEM((steps_top + 1,), jnp.int32),
            pltpu.SMEM((slots,), jnp.int32),
            pltpu.SMEM((slots,), jnp.int32),
            pltpu.SMEM((slots,), jnp.int32),
            pltpu.SemaphoreType.DMA((4,)),
        ],
        compiler_params=pltpu.CompilerParams(vmem_limit_bytes=56 * 1024 * 1024),
        name="layers",
    )(lengths, parity, tokens, cot, gains, shifts, wqkv, qvb, wout, outb, wup, upb, wdown)


AXES = ("dp", "group")


def finish_kernel(parity, mine, other, gains, shifts, qkv, qvb, out, outb, up, upb, down):
    width = mine.shape[1]
    hidden = up.shape[2]
    for p in range(LAYERS):

        @pl.when(parity[0] == p)
        def _():
            for l in range(LAYERS):
                src = mine if l == p else other
                at = 0
                for c in range(3):
                    qkv[l, :, c * width:(c + 1) * width] = src[at:at + width, :].astype(f32)
                    at += width
                out[l] = src[at:at + width, :].astype(f32)
                at += width
                for c in range(hidden // width):
                    up[l, :, c * width:(c + 1) * width] = src[at:at + width, :].astype(f32)
                    at += width
                down[l] = src[at:at + hidden, :].astype(f32)
                at += hidden
                small = src[at:at + SMALL, :].astype(f32)
                gains[l] = small[0:2]
                shifts[l] = small[2:4]
                qvb[l] = small[4:6]
                outb[l] = small[6:8]
                for c in range(hidden // width):
                    upb[l:l + 1, c * width:(c + 1) * width] = small[8 + c:9 + c]


def finish_call(parity, mine, other, args):
    vm = pl.BlockSpec(memory_space=pltpu.VMEM)
    sm = pl.BlockSpec(memory_space=pltpu.SMEM)
    return pl.pallas_call(
        finish_kernel,
        out_shape=tuple(jax.ShapeDtypeStruct(a.shape, f32) for a in args[2:11]),
        in_specs=[sm, vm, vm],
        out_specs=(vm,) * 9,
        compiler_params=pltpu.CompilerParams(vmem_limit_bytes=16 * 1024 * 1024),
        name="finish",
    )(parity, mine, other)


def exchange(x, bits, devices):
    return lax.ppermute(x, AXES, [(i, i ^ bits[i % 2]) for i in range(devices)])


def added(a, b):
    return (a.astype(f32) + b.astype(f32)).astype(bf16)


def all_sum(mine, other, index, devices):
    x = added(mine, exchange(other, (1, 1), devices))
    bits = [1 << i for i in range(1, devices.bit_length() - 1)]
    crossed = list(bits)
    for i in range(0, len(bits) - 1, 2):
        crossed[i], crossed[i + 1] = bits[i + 1], bits[i]
    steps = list(zip(bits, crossed))
    turn = len(steps) // 2
    orders = [steps, steps[turn:] + steps[:turn]]
    size = x.shape[0] // len(orders)
    parts = [x[i * size:(i + 1) * size] for i in range(len(orders))]
    lows = [(index // jnp.where(index % 2 == 0, order[0][0], order[0][1])) % 2 == 0 for order in orders]
    half = size // 2
    kept = [jnp.where(low, p[:half], p[half:]) for p, low in zip(parts, lows)]
    sent = [jnp.where(low, p[half:], p[:half]) for p, low in zip(parts, lows)]
    for step in range(len(steps)):
        got = [exchange(p, order[step], devices) for p, order in zip(sent, orders)]
        kept = [added(p, q) for p, q in zip(kept, got)]
        sent = kept
    got = [exchange(p, order[0], devices) for p, order in zip(kept, orders)]
    parts = [
        jnp.where(low, jnp.concatenate([p, q]), jnp.concatenate([q, p]))
        for p, q, low in zip(kept, got, lows)
    ]
    x = jnp.concatenate(parts)
    return x, exchange(x, (1, 1), devices)


def solution(mesh):
    mesh_shape = dict(mesh.shape)
    devices = mesh_shape["dp"] * mesh_shape["group"]

    def per_device(*args):
        index = lax.axis_index("dp") * mesh_shape["group"] + lax.axis_index("group")
        parity = (index % 2).astype(jnp.int32).reshape(1)
        output, grad_tokens, mine, other = main_call(args, STEPS, parity)
        mine, other = all_sum(mine, other, index, devices)
        return (output, grad_tokens) + tuple(finish_call(parity, mine, other, args))

    rows = P(AXES, None, None)
    return jax.shard_map(
        per_device,
        mesh=mesh,
        in_specs=(rows, P(AXES)) + (P(),) * 9 + (rows,),
        out_specs=(rows, rows) + (P(),) * 9,
        check_vma=False,
    )
```

```python
import functools
import jax
import jax.numpy as jnp
from jax import lax
from jax.sharding import PartitionSpec as P
from jax.experimental import pallas as pl
from jax.experimental.pallas import tpu as pltpu

STEPS = 30
HEAD = 16
LAYERS = 2
BIN = 128
SMALL = 64
FWD_GROUP = 1
BWD_GROUP = 4
MEMBERS = 2
UNIT_BINS = 8
eps = 1e-05
dead_score = -1e30
LOG2E = 1.4426950408889634
LN2 = 0.6931471805599453
GELU_C = 0.7978845608
GELU_K = 0.044715
bf16 = jnp.bfloat16
f32 = jnp.float32


def dot(a, b):
    return lax.dot_general(a, b, (((1,), (0,)), ((), ())), preferred_element_type=f32)


def dot_nt(a, b):
    return lax.dot_general(a, b, (((1,), (1,)), ((), ())), preferred_element_type=f32)


def plan(lengths, order, count, mem_traj, mem_off, mem_len, steps_top):
    trajs = lengths.shape[0]
    pairs = trajs // 2

    def clear(i, c):
        count[i] = 0
        return c

    lax.fori_loop(0, steps_top + 1, clear, 0, unroll=True)

    def tally(t, c):
        s = lengths[t] // 3
        count[s] = count[s] + 1
        return c

    lax.fori_loop(0, trajs, tally, 0, unroll=4)

    def prefix(i, total):
        s = steps_top - i
        n = count[s]
        count[s] = total
        return total + n

    lax.fori_loop(0, steps_top + 1, prefix, 0, unroll=True)

    def rank(t, c):
        s = lengths[t] // 3
        p = count[s]
        order[p] = t
        count[s] = p + 1
        return c

    lax.fori_loop(0, trajs, rank, 0, unroll=4)

    def member(slot, t, offset, length):
        mem_traj[slot] = t
        mem_off[slot] = offset
        mem_len[slot] = length

    def pair(p, nbins):
        long, short = order[p], order[trajs - 1 - p]
        length, length_two = lengths[long], lengths[short]
        fits = length + length_two <= BIN
        member(2 * p, long, 0, length)
        member(2 * p + 1, short, length, jnp.where(fits, length_two, 0))
        member(2 * nbins, short, 0, length_two)
        member(2 * nbins + 1, short, length_two, 0)
        return nbins + jnp.where(fits, 0, 1)

    nbins = lax.fori_loop(0, pairs, pair, pairs)
    units = (nbins + UNIT_BINS - 1) // UNIT_BINS

    def pad(i, c):
        member(i, 0, BIN, 0)
        return c

    lax.fori_loop(2 * nbins, 2 * UNIT_BINS * units, pad, 0)
    return units


def norm_parts(x):
    c = x - jnp.mean(x, -1, keepdims=True)
    rstd = lax.rsqrt(jnp.mean(c * c, -1, keepdims=True) + eps)
    return c * rstd, rstd


def norm_back(dy, normed, rstd, gain):
    dg = dy * gain
    return (dg - jnp.mean(dg, -1, keepdims=True) - normed * jnp.mean(dg * normed, -1, keepdims=True)) * rstd


def head_masks(width):
    lane = lax.broadcasted_iota(jnp.int32, (1, width), 1) // HEAD
    return [jnp.where(lane == h, 1.0, 0.0).astype(bf16) for h in range(width // HEAD)]


def row_sum(x):
    return jnp.sum(x, 0, keepdims=True)


def main_kernel(
    lengths, parity, tok_hbm, cot_hbm, gains_hbm, shifts_hbm, wqkv_hbm, qvb_hbm, wout_hbm, outb_hbm, wup_hbm, upb_hbm, wdown_hbm,
    out_hbm, gtok_hbm, mine_a, mine_b, other_a, other_b,
    tok, cot, gains, shifts, wqkv, qvb, wout, outb, wup, upb, wdown, out, gtok, gsum,
    a_qkv, a_out, a_up, a_down, a_small, e_scr, act_scr, gp_scr,
    order, count, mem_traj, mem_off, mem_len, sems,
    *, steps_top,
):
    trajs, slot_rows, width = tok.shape
    hidden = wup.shape[2]
    heads = width // HEAD
    pairs = heads // 2
    unit = BIN * UNIT_BINS
    sources = (tok_hbm, cot_hbm, gains_hbm, shifts_hbm, wqkv_hbm, qvb_hbm, wout_hbm, outb_hbm, wup_hbm, upb_hbm, wdown_hbm)
    targets = (tok, cot, gains, shifts, wqkv, qvb, wout, outb, wup, upb, wdown)
    loads = [pltpu.make_async_copy(a, b, sems.at[i]) for i, (a, b) in enumerate(zip(sources, targets))]
    for copy in loads:
        copy.start()
    for ref in (a_qkv, a_out, a_up, a_down, a_small):
        ref[...] = jnp.zeros_like(ref)
    units = plan(lengths, order, count, mem_traj, mem_off, mem_len, steps_top)
    for copy in loads:
        copy.wait()

    masks = head_masks(width)
    mask_pairs = [
        jnp.concatenate([jnp.broadcast_to(masks[2 * j], (BIN, width)), jnp.broadcast_to(masks[2 * j + 1], (BIN, width))], 0)
        for j in range(pairs)
    ]

    def pair_rows(x, j):
        return jnp.concatenate([x * masks[2 * j], x * masks[2 * j + 1]], 0)

    blank = jnp.zeros((HEAD, BIN), bf16)
    ones = jnp.ones((HEAD, BIN), bf16)

    def pair_columns(xt, j):
        lo, mid, hi = 2 * j * HEAD, (2 * j + 1) * HEAD, (2 * j + 2) * HEAD
        parts = [
            jnp.concatenate([xt[lo:mid], blank], 1),
            jnp.concatenate([blank, xt[mid:hi]], 1),
        ]
        if j > 0:
            parts = [jnp.zeros((lo, 2 * BIN), bf16)] + parts
        if hi < width:
            parts = parts + [jnp.zeros((width - hi, 2 * BIN), bf16)]
        return jnp.concatenate(parts, 0)

    ones_t = jnp.ones((width, BIN), bf16)
    mask_columns = [pair_columns(ones_t, j) for j in range(pairs)]

    def body(u, carry):
        q_iota = lax.broadcasted_iota(jnp.int32, (BIN, BIN), 0)
        k_iota = lax.broadcasted_iota(jnp.int32, (BIN, BIN), 1)
        toks, cots, biases = [], [], []
        for b in range(UNIT_BINS):
            picks, rows_in = [], []
            start = jnp.zeros((BIN, BIN), jnp.int32)
            for m in range(MEMBERS):
                slot = (u * UNIT_BINS + b) * MEMBERS + m
                t, o, n = mem_traj[slot], mem_off[slot], mem_len[slot]
                picks.append(jnp.where((q_iota - o == k_iota) & (k_iota < n), 1.0, 0.0).astype(bf16))
                rows_in += [jnp.concatenate([tok[t], cot[t]], axis=1), jnp.zeros((BIN - slot_rows, 2 * width), bf16)]
                start = jnp.where(q_iota >= o + n, o + n, start)
            x = dot(jnp.concatenate(picks, 1), jnp.concatenate(rows_in, 0))
            toks.append(x[:, :width])
            cots.append(x[:, width:])
            biases.append(jnp.where((k_iota <= q_iota) & (k_iota >= start), 0.0, dead_score))
        x = jnp.concatenate(toks, 0)
        g = jnp.concatenate(cots, 0)
        row = lax.broadcasted_iota(jnp.int32, (unit, 1), 0) % BIN
        factor = jnp.where(row % 3 == 0, 0.5, 1.0)
        x = x * factor

        saved = []
        for l in range(LAYERS):
            n1, rstd1 = norm_parts(x)
            h1 = (n1 * gains[l, 0:1, :] + shifts[l, 0:1, :]).astype(bf16)
            joint = dot(h1, wqkv[l])
            q = ((joint[:, :width] + qvb[l, 0:1, :]) * (LOG2E * HEAD ** -0.5)).astype(bf16)
            k = joint[:, width:2 * width].astype(bf16)
            v = (joint[:, 2 * width:] + qvb[l, 1:2, :]).astype(bf16)
            rows_of = [slice(b * BIN, (b + 1) * BIN) for b in range(UNIT_BINS)]
            mixed_bins, rl_bins = [], []
            for first in range(0, UNIT_BINS, FWD_GROUP):
                bins = range(first, first + FWD_GROUP)
                acc = {b: None for b in bins}

                def scores(j):
                    return {b: dot_nt(q[rows_of[b]], pair_rows(k[rows_of[b]], j)) for b in bins}

                ahead = scores(0)
                for j in range(pairs):
                    s = ahead
                    if j + 1 < pairs:
                        ahead = scores(j + 1)
                    es = {}
                    for b in bins:
                        halves = []
                        for half in range(2):
                            sh = s[b][:, half * BIN:(half + 1) * BIN] + biases[b]
                            halves.append(jnp.exp2(sh - jnp.max(sh, -1, keepdims=True)).astype(bf16))
                        es[b] = jnp.concatenate(halves, 1)
                        e_scr[l, rows_of[b], 2 * j * BIN:(2 * j + 2) * BIN] = es[b]
                    for b in bins:
                        part = dot(es[b], jnp.concatenate([pair_rows(v[rows_of[b]], j), mask_pairs[j]], 1))
                        acc[b] = part if acc[b] is None else acc[b] + part
                for b in bins:
                    rl = 1.0 / acc[b][:, width:]
                    mixed_bins.append((acc[b][:, :width] * rl).astype(bf16))
                    rl_bins.append(rl)
            mixed = jnp.concatenate(mixed_bins, 0)
            rl = jnp.concatenate(rl_bins, 0)
            x1 = x + dot(mixed, wout[l]) + outb[l, 0:1, :]
            n2, rstd2 = norm_parts(x1)
            h2 = (n2 * gains[l, 1:2, :] + shifts[l, 1:2, :]).astype(bf16)
            hid = dot(h2, wup[l]) + upb[l:l + 1, :]
            sq = hid * hid
            w = 0.5 * jnp.tanh(hid * (GELU_C + (GELU_C * GELU_K) * sq)) + 0.5
            act = hid * w
            gp = w + (act * (1.0 - w)) * (2 * GELU_C + (6 * GELU_C * GELU_K) * sq)
            act_b = act.astype(bf16)
            act_scr[l] = act_b
            gp_scr[l] = gp.astype(bf16)
            saved.append((n1, rstd1, h1, q, k, v, mixed, rl, n2, rstd2, h2))
            x = x1 + dot(act_b, wdown[l]) + outb[l, 1:2, :]

        out_b = x.astype(bf16)
        for l in reversed(range(LAYERS)):
            n1, rstd1, h1, q, k, v, mixed, rl, n2, rstd2, h2 = saved[l]
            e2 = g.astype(bf16)
            a_small[l, 7:8, :] += row_sum(e2.astype(f32))
            du = (dot_nt(e2, wdown[l]) * gp_scr[l].astype(f32)).astype(bf16)
            dh2 = dot_nt(du, wup[l])
            a_down[l] += dot(e2.T, act_scr[l])
            a_up[l] += dot(h2.T, du)
            dus = row_sum(du.astype(f32))
            for c in range(hidden // width):
                a_small[l, 8 + c:9 + c, :] += dus[:, c * width:(c + 1) * width]
            a_small[l, 1:2, :] += row_sum(dh2 * n2)
            a_small[l, 3:4, :] += row_sum(dh2)
            g1 = g + norm_back(dh2, n2, rstd2, gains[l, 1:2, :])
            e1 = g1.astype(bf16)
            dm = dot_nt(e1, wout[l])
            a_out[l] += dot(mixed.T, e1)
            a_small[l, 6:7, :] += row_sum(e1.astype(f32))
            dm1 = dm * rl
            dmo = -(dm1 * mixed.astype(f32))
            dm1 = dm1.astype(bf16)
            dmo = dmo.astype(bf16)
            rows_of = [slice(b * BIN, (b + 1) * BIN) for b in range(UNIT_BINS)]
            dqkv_bins = []
            for first in range(0, UNIT_BINS, BWD_GROUP):
                bins = range(first, first + BWD_GROUP)
                lhs = {b: jnp.concatenate([dm1[rows_of[b]], dmo[rows_of[b]]], 1) for b in bins}
                dm_t = {b: dm1[rows_of[b]].T for b in bins}
                q_t = {b: q[rows_of[b]].T for b in bins}
                v_t = {b: v[rows_of[b]].T for b in bins}
                dq = {b: None for b in bins}
                dv_t = {b: [] for b in bins}
                dk_t = {b: [] for b in bins}

                def d_scores(j):
                    return {b: dot(lhs[b], jnp.concatenate([pair_columns(v_t[b], j), mask_columns[j]], 0)) for b in bins}

                ahead = d_scores(0)
                for j in range(pairs):
                    top, low = 2 * j * HEAD, (2 * j + 2) * HEAD
                    z = ahead
                    if j + 1 < pairs:
                        ahead = d_scores(j + 1)
                    es = {b: e_scr[l, rows_of[b], 2 * j * BIN:(2 * j + 2) * BIN] for b in bins}
                    for b in bins:
                        pv = dot(dm_t[b][top:low], es[b])
                        dv_t[b] += [pv[:HEAD, :BIN], pv[HEAD:, BIN:]]
                    ds = {b: es[b] * z[b].astype(bf16) for b in bins}
                    for b in bins:
                        part = dot(ds[b], pair_rows(k[rows_of[b]], j))
                        dq[b] = part if dq[b] is None else dq[b] + part
                    for b in bins:
                        pk = dot(q_t[b][top:low], ds[b])
                        dk_t[b] += [pk[:HEAD, :BIN], pk[HEAD:, BIN:]]
                for b in bins:
                    dv = jnp.concatenate(dv_t[b], 0).T
                    dk = jnp.concatenate(dk_t[b], 0).T * LN2
                    dqkv_bins.append(jnp.concatenate([(dq[b] * HEAD ** -0.5).astype(bf16), dk.astype(bf16), dv.astype(bf16)], 1))
            dqkv = jnp.concatenate(dqkv_bins, 0)
            dh = dot_nt(dqkv, wqkv[l])
            a_qkv[l] += dot(h1.T, dqkv)
            sums = row_sum(dqkv.astype(f32))
            a_small[l, 4:5, :] += sums[:, :width]
            a_small[l, 5:6, :] += sums[:, 2 * width:]
            a_small[l, 0:1, :] += row_sum(dh * n1)
            a_small[l, 2:3, :] += row_sum(dh)
            g = g1 + norm_back(dh, n1, rstd1, gains[l, 0:1, :])

        grad_b = (g * factor).astype(bf16)
        s_iota = lax.broadcasted_iota(jnp.int32, (slot_rows, BIN), 0)
        p_iota = lax.broadcasted_iota(jnp.int32, (slot_rows, BIN), 1)
        both = jnp.concatenate([out_b, grad_b], 1)
        for b in range(UNIT_BINS):
            homes, picks = [], []
            for m in range(MEMBERS):
                slot = (u * UNIT_BINS + b) * MEMBERS + m
                t, o, n = mem_traj[slot], mem_off[slot], mem_len[slot]
                picks.append(jnp.where((p_iota - o == s_iota) & (s_iota < n), 1.0, 0.0).astype(bf16))
                homes.append(jnp.where(n > 0, t, trajs))
            rows = dot(jnp.concatenate(picks, 0), both[b * BIN:(b + 1) * BIN]).astype(bf16)
            for m, home in enumerate(homes):
                out[home] = rows[m * slot_rows:(m + 1) * slot_rows, :width]
                gtok[home] = rows[m * slot_rows:(m + 1) * slot_rows, width:]
        return carry

    lax.fori_loop(0, units, body, 0)

    stores = [
        pltpu.make_async_copy(out.at[pl.ds(0, trajs)], out_hbm, sems.at[0]),
        pltpu.make_async_copy(gtok.at[pl.ds(0, trajs)], gtok_hbm, sems.at[1]),
    ]
    for copy in stores:
        copy.start()
    for l in range(LAYERS):
        at = 0
        for c in range(3):
            gsum[l, at:at + width, :] = a_qkv[l, :, c * width:(c + 1) * width].astype(bf16)
            at += width
        gsum[l, at:at + width, :] = a_out[l].astype(bf16)
        at += width
        for c in range(hidden // width):
            gsum[l, at:at + width, :] = a_up[l, :, c * width:(c + 1) * width].astype(bf16)
            at += width
        for c in range(hidden // width):
            gsum[l, at:at + width, :] = a_down[l, :, c * width:(c + 1) * width].T.astype(bf16)
            at += width
        gsum[l, at:at + SMALL, :] = a_small[l].astype(bf16)
    mine = parity[0]
    half = gsum.shape[1] // 2
    stores += [
        pltpu.make_async_copy(gsum.at[l, pl.ds(i * half, half)], to, sems.at[2 + 2 * k + i])
        for k, (l, pair) in enumerate(((1 - mine, (other_a, other_b)), (mine, (mine_a, mine_b))))
        for i, to in enumerate(pair)
    ]
    for copy in stores[2:]:
        copy.start()
    for copy in stores:
        copy.wait()


def main_call(args, steps_top, parity):
    tokens, lengths, gains, shifts, wqkv, qvb, wout, outb, wup, upb, wdown, cot = args
    trajs, slot_rows, width = tokens.shape
    hidden = wup.shape[2]
    unit = BIN * UNIT_BINS
    slots = 2 * (trajs + UNIT_BINS)
    per_layer = 4 * width + 2 * hidden + SMALL
    sm = pl.BlockSpec(memory_space=pltpu.SMEM)
    hbm = pl.BlockSpec(memory_space=pl.ANY)
    sums = jax.ShapeDtypeStruct((per_layer // 2, width), bf16)
    return pl.pallas_call(
        functools.partial(main_kernel, steps_top=steps_top),
        out_shape=(
            jax.ShapeDtypeStruct(tokens.shape, bf16),
            jax.ShapeDtypeStruct(tokens.shape, bf16),
            sums,
            sums,
            sums,
            sums,
        ),
        in_specs=[sm, sm] + [hbm] * 11,
        out_specs=(hbm,) * 6,
        scratch_shapes=[
            pltpu.VMEM(tokens.shape, bf16),
            pltpu.VMEM(tokens.shape, bf16),
        ]
        + [pltpu.VMEM(a.shape, a.dtype) for a in (gains, shifts, wqkv, qvb, wout, outb, wup, upb, wdown)]
        + [
            pltpu.VMEM((trajs + 1, slot_rows, width), bf16),
            pltpu.VMEM((trajs + 1, slot_rows, width), bf16),
            pltpu.VMEM((LAYERS, per_layer, width), bf16),
            pltpu.VMEM((LAYERS, width, 3 * width), f32),
            pltpu.VMEM((LAYERS, width, width), f32),
            pltpu.VMEM((LAYERS, width, hidden), f32),
            pltpu.VMEM((LAYERS, width, hidden), f32),
            pltpu.VMEM((LAYERS, SMALL, width), f32),
            pltpu.VMEM((LAYERS, unit, width // HEAD * BIN), bf16),
            pltpu.VMEM((LAYERS, unit, hidden), bf16),
            pltpu.VMEM((LAYERS, unit, hidden), bf16),
            pltpu.SMEM((trajs,), jnp.int32),
            pltpu.SMEM((steps_top + 1,), jnp.int32),
            pltpu.SMEM((slots,), jnp.int32),
            pltpu.SMEM((slots,), jnp.int32),
            pltpu.SMEM((slots,), jnp.int32),
            pltpu.SemaphoreType.DMA((11,)),
        ],
        compiler_params=pltpu.CompilerParams(vmem_limit_bytes=56 * 1024 * 1024),
        name="layers",
    )(lengths, parity, tokens, cot, gains, shifts, wqkv, qvb, wout, outb, wup, upb, wdown)


AXES = ("dp", "group")


def finish_kernel(parity, mine_a, mine_b, other_a, other_b, gains, shifts, qkv, qvb, out, outb, up, upb, down):
    rows, width = mine_a.shape
    hidden = up.shape[2]
    for p in range(LAYERS):

        @pl.when(parity[0] == p)
        def _():
            for l in range(LAYERS):
                pieces = (mine_a, mine_b) if l == p else (other_a, other_b)

                def take(at, count):
                    found = []
                    while count > 0:
                        piece, first = divmod(at, rows)
                        now = min(count, rows - first)
                        found.append(pieces[piece][first:first + now, :].astype(f32))
                        at, count = at + now, count - now
                    return found[0] if len(found) == 1 else jnp.concatenate(found, 0)

                at = 0
                for c in range(3):
                    qkv[l, :, c * width:(c + 1) * width] = take(at, width)
                    at += width
                out[l] = take(at, width)
                at += width
                for c in range(hidden // width):
                    up[l, :, c * width:(c + 1) * width] = take(at, width)
                    at += width
                down[l] = take(at, hidden)
                at += hidden
                small = take(at, SMALL)
                gains[l] = small[0:2]
                shifts[l] = small[2:4]
                qvb[l] = small[4:6]
                outb[l] = small[6:8]
                for c in range(hidden // width):
                    upb[l:l + 1, c * width:(c + 1) * width] = small[8 + c:9 + c]


def finish_call(parity, mine, other, args):
    vm = pl.BlockSpec(memory_space=pltpu.VMEM)
    sm = pl.BlockSpec(memory_space=pltpu.SMEM)
    return pl.pallas_call(
        finish_kernel,
        out_shape=tuple(jax.ShapeDtypeStruct(a.shape, f32) for a in args[2:11]),
        in_specs=[sm] + [vm] * 4,
        out_specs=(vm,) * 9,
        compiler_params=pltpu.CompilerParams(vmem_limit_bytes=16 * 1024 * 1024),
        name="finish",
    )(parity, *mine, *other)


def exchange(x, bits, devices):
    return lax.ppermute(x, AXES, [(i, i ^ bits[i % 2]) for i in range(devices)])


def added(a, b):
    return (a.astype(f32) + b.astype(f32)).astype(bf16)


def all_sum(mine, other, index, devices):
    bits = [1 << i for i in range(1, devices.bit_length() - 1)]
    crossed = list(bits)
    for i in range(0, len(bits) - 1, 2):
        crossed[i], crossed[i + 1] = bits[i + 1], bits[i]
    steps = list(zip(bits, crossed))
    order = []
    for i in range(0, len(steps), 4):
        some = steps[i:i + 4]
        order += some[0::2] + some[1::2]
    turned = list(order)
    for i in range(0, len(order) - 1, 2):
        turned[i], turned[i + 1] = order[i + 1], order[i]
    orders = [order, turned]
    parts = [added(m, exchange(o, (1, 1), devices)) for m, o in zip(mine, other)]
    lows = [(index // jnp.where(index % 2 == 0, order[0][0], order[0][1])) % 2 == 0 for order in orders]
    half = parts[0].shape[0] // 2
    kept = [jnp.where(low, p[:half], p[half:]) for p, low in zip(parts, lows)]
    sent = [jnp.where(low, p[half:], p[:half]) for p, low in zip(parts, lows)]
    for step in range(len(steps)):
        got = [exchange(p, order[step], devices) for p, order in zip(sent, orders)]
        kept = [added(p, q) for p, q in zip(kept, got)]
        sent = kept
    got = [exchange(p, order[0], devices) for p, order in zip(kept, orders)]
    parts = [
        jnp.where(low, jnp.concatenate([p, q]), jnp.concatenate([q, p]))
        for p, q, low in zip(kept, got, lows)
    ]
    return parts, [exchange(p, (1, 1), devices) for p in parts]


def solution(mesh):
    mesh_shape = dict(mesh.shape)
    devices = mesh_shape["dp"] * mesh_shape["group"]

    def per_device(*args):
        index = lax.axis_index("dp") * mesh_shape["group"] + lax.axis_index("group")
        parity = (index % 2).astype(jnp.int32).reshape(1)
        output, grad_tokens, mine_a, mine_b, other_a, other_b = main_call(args, STEPS, parity)
        mine, other = all_sum((mine_a, mine_b), (other_a, other_b), index, devices)
        return (output, grad_tokens) + tuple(finish_call(parity, mine, other, args))

    rows = P(AXES, None, None)
    return jax.shard_map(
        per_device,
        mesh=mesh,
        in_specs=(rows, P(AXES)) + (P(),) * 9 + (rows,),
        out_specs=(rows, rows) + (P(),) * 9,
        check_vma=False,
    )
```

```python
import functools
import jax
import jax.numpy as jnp
from jax import lax
from jax.sharding import PartitionSpec as P
from jax.experimental import pallas as pl
from jax.experimental.pallas import tpu as pltpu

STEPS = 30
HEAD = 16
LAYERS = 2
BIN = 128
SMALL = 64
FWD_GROUP = 1
BWD_GROUP = 4
MEMBERS = 2
UNIT_BINS = 8
eps = 1e-05
dead_score = -1e30
LOG2E = 1.4426950408889634
LN2 = 0.6931471805599453
GELU_C = 0.7978845608
GELU_K = 0.044715
bf16 = jnp.bfloat16
f32 = jnp.float32


def dot(a, b):
    return lax.dot_general(a, b, (((1,), (0,)), ((), ())), preferred_element_type=f32)


def dot_nt(a, b):
    return lax.dot_general(a, b, (((1,), (1,)), ((), ())), preferred_element_type=f32)


def plan(lengths, order, count, mem_traj, mem_off, mem_len, steps_top):
    trajs = lengths.shape[0]
    pairs = trajs // 2

    def clear(i, c):
        count[i] = 0
        return c

    lax.fori_loop(0, steps_top + 1, clear, 0, unroll=True)

    def tally(t, c):
        s = lengths[t] // 3
        count[s] = count[s] + 1
        return c

    lax.fori_loop(0, trajs, tally, 0, unroll=4)

    def prefix(i, total):
        s = steps_top - i
        n = count[s]
        count[s] = total
        return total + n

    lax.fori_loop(0, steps_top + 1, prefix, 0, unroll=True)

    def rank(t, c):
        s = lengths[t] // 3
        p = count[s]
        order[p] = t
        count[s] = p + 1
        return c

    lax.fori_loop(0, trajs, rank, 0, unroll=4)

    def member(slot, t, offset, length):
        mem_traj[slot] = t
        mem_off[slot] = offset
        mem_len[slot] = length

    def pair(p, nbins):
        long, short = order[p], order[trajs - 1 - p]
        length, length_two = lengths[long], lengths[short]
        fits = length + length_two <= BIN
        member(2 * p, long, 0, length)
        member(2 * p + 1, short, length, jnp.where(fits, length_two, 0))
        member(2 * nbins, short, 0, length_two)
        member(2 * nbins + 1, short, length_two, 0)
        return nbins + jnp.where(fits, 0, 1)

    nbins = lax.fori_loop(0, pairs, pair, pairs)
    units = (nbins + UNIT_BINS - 1) // UNIT_BINS

    def pad(i, c):
        member(i, 0, BIN, 0)
        return c

    lax.fori_loop(2 * nbins, 2 * UNIT_BINS * units, pad, 0)
    return units


def norm_parts(x):
    c = x - jnp.mean(x, -1, keepdims=True)
    rstd = lax.rsqrt(jnp.mean(c * c, -1, keepdims=True) + eps)
    return c * rstd, rstd


def norm_back(dy, normed, rstd, gain):
    dg = dy * gain
    return (dg - jnp.mean(dg, -1, keepdims=True) - normed * jnp.mean(dg * normed, -1, keepdims=True)) * rstd


def head_masks(width):
    lane = lax.broadcasted_iota(jnp.int32, (1, width), 1) // HEAD
    return [jnp.where(lane == h, 1.0, 0.0).astype(bf16) for h in range(width // HEAD)]


def row_sum(x):
    return jnp.sum(x, 0, keepdims=True)


def main_kernel(
    lengths, parity, tok_hbm, cot_hbm, gains_hbm, shifts_hbm, wqkv_hbm, qvb_hbm, wout_hbm, outb_hbm, wup_hbm, upb_hbm, wdown_hbm,
    out_hbm, gtok_hbm, mine_a, mine_b, other_a, other_b,
    tok, cot, gains, shifts, wqkv, qvb, wout, outb, wup, upb, wdown, out, gtok, gsum,
    a_qkv, a_out, a_up, a_down, a_small, e_scr, act_scr, gp_scr, half_up, half_down,
    order, count, mem_traj, mem_off, mem_len, sems,
    *, steps_top,
):
    trajs, slot_rows, width = tok.shape
    hidden = wup.shape[2]
    heads = width // HEAD
    pairs = heads // 2
    unit = BIN * UNIT_BINS
    sources = (tok_hbm, cot_hbm, gains_hbm, shifts_hbm, wqkv_hbm, qvb_hbm, wout_hbm, outb_hbm, wup_hbm, upb_hbm, wdown_hbm)
    targets = (tok, cot, gains, shifts, wqkv, qvb, wout, outb, wup, upb, wdown)
    loads = [pltpu.make_async_copy(a, b, sems.at[i]) for i, (a, b) in enumerate(zip(sources, targets))]
    for copy in loads:
        copy.start()
    for ref in (a_qkv, a_out, a_up, a_down, a_small):
        ref[...] = jnp.zeros_like(ref)
    units = plan(lengths, order, count, mem_traj, mem_off, mem_len, steps_top)
    for copy in loads:
        copy.wait()

    at = lax.broadcasted_iota(jnp.int32, (width, hidden), 0)
    for l in range(LAYERS):
        bias = 0.5 * upb[l:l + 1, :]
        high = bias.astype(bf16).astype(f32)
        half_up[l, :width, :] = wup[l] * jnp.asarray(0.5, bf16)
        half_up[l, width:, :] = jnp.where(at == 0, high, jnp.where(at == 1, bias - high, 0.0)).astype(bf16)
        half_down[l] = wdown[l] * jnp.asarray(0.5, bf16)

    masks = head_masks(width)
    mask_pairs = [
        jnp.concatenate([jnp.broadcast_to(masks[2 * j], (BIN, width)), jnp.broadcast_to(masks[2 * j + 1], (BIN, width))], 0)
        for j in range(pairs)
    ]

    def pair_rows(x, j):
        return jnp.concatenate([x * masks[2 * j], x * masks[2 * j + 1]], 0)

    blank = jnp.zeros((HEAD, BIN), bf16)
    ones = jnp.ones((HEAD, BIN), bf16)

    def pair_columns(xt, j):
        lo, mid, hi = 2 * j * HEAD, (2 * j + 1) * HEAD, (2 * j + 2) * HEAD
        parts = [
            jnp.concatenate([xt[lo:mid], blank], 1),
            jnp.concatenate([blank, xt[mid:hi]], 1),
        ]
        if j > 0:
            parts = [jnp.zeros((lo, 2 * BIN), bf16)] + parts
        if hi < width:
            parts = parts + [jnp.zeros((width - hi, 2 * BIN), bf16)]
        return jnp.concatenate(parts, 0)

    ones_t = jnp.ones((width, BIN), bf16)
    mask_columns = [pair_columns(ones_t, j) for j in range(pairs)]

    lane = lax.broadcasted_iota(jnp.int32, (unit, width), 1)
    ones_rows = jnp.ones((16, unit), bf16)
    ones_lanes = jnp.where(lane < 2, 1.0, 0.0).astype(bf16)

    def body(u, carry):
        q_iota = lax.broadcasted_iota(jnp.int32, (BIN, BIN), 0)
        k_iota = lax.broadcasted_iota(jnp.int32, (BIN, BIN), 1)
        toks, cots, biases = [], [], []
        for b in range(UNIT_BINS):
            picks, rows_in = [], []
            start = jnp.zeros((BIN, BIN), jnp.int32)
            for m in range(MEMBERS):
                slot = (u * UNIT_BINS + b) * MEMBERS + m
                t, o, n = mem_traj[slot], mem_off[slot], mem_len[slot]
                picks.append(jnp.where((q_iota - o == k_iota) & (k_iota < n), 1.0, 0.0).astype(bf16))
                rows_in += [jnp.concatenate([tok[t], cot[t]], axis=1), jnp.zeros((BIN - slot_rows, 2 * width), bf16)]
                start = jnp.where(q_iota >= o + n, o + n, start)
            x = dot(jnp.concatenate(picks, 1), jnp.concatenate(rows_in, 0))
            toks.append(x[:, :width])
            cots.append(x[:, width:])
            biases.append(jnp.where((k_iota <= q_iota) & (k_iota >= start), 0.0, dead_score))
        x = jnp.concatenate(toks, 0)
        g = jnp.concatenate(cots, 0)
        row = lax.broadcasted_iota(jnp.int32, (unit, 1), 0) % BIN
        factor = jnp.where(row % 3 == 0, 0.5, 1.0)
        x = x * factor

        saved = []
        for l in range(LAYERS):
            n1, rstd1 = norm_parts(x)
            h1 = (n1 * gains[l, 0:1, :] + shifts[l, 0:1, :]).astype(bf16)
            joint = dot(h1, wqkv[l])
            q = ((joint[:, :width] + qvb[l, 0:1, :]) * (LOG2E * HEAD ** -0.5)).astype(bf16)
            k = joint[:, width:2 * width].astype(bf16)
            v = (joint[:, 2 * width:] + qvb[l, 1:2, :]).astype(bf16)
            rows_of = [slice(b * BIN, (b + 1) * BIN) for b in range(UNIT_BINS)]
            mixed_bins, rl_bins = [], []
            for first in range(0, UNIT_BINS, FWD_GROUP):
                bins = range(first, first + FWD_GROUP)
                acc = {b: None for b in bins}

                def scores(j):
                    return {b: dot_nt(q[rows_of[b]], pair_rows(k[rows_of[b]], j)) for b in bins}

                ahead = scores(0)
                for j in range(pairs):
                    s = ahead
                    if j + 1 < pairs:
                        ahead = scores(j + 1)
                    es = {}
                    for b in bins:
                        halves = []
                        for half in range(2):
                            sh = s[b][:, half * BIN:(half + 1) * BIN] + biases[b]
                            halves.append(jnp.exp2(sh - jnp.max(sh, -1, keepdims=True)).astype(bf16))
                        es[b] = jnp.concatenate(halves, 1)
                        e_scr[l, rows_of[b], 2 * j * BIN:(2 * j + 2) * BIN] = es[b]
                    for b in bins:
                        part = dot(es[b], jnp.concatenate([pair_rows(v[rows_of[b]], j), mask_pairs[j]], 1))
                        acc[b] = part if acc[b] is None else acc[b] + part
                for b in bins:
                    rl = 1.0 / acc[b][:, width:]
                    mixed_bins.append((acc[b][:, :width] * rl).astype(bf16))
                    rl_bins.append(rl)
            mixed = jnp.concatenate(mixed_bins, 0)
            rl = jnp.concatenate(rl_bins, 0)
            x1 = x + dot(mixed, wout[l]) + outb[l, 0:1, :]
            n2, rstd2 = norm_parts(x1)
            h2 = (n2 * gains[l, 1:2, :] + shifts[l, 1:2, :]).astype(bf16)
            hid = dot(jnp.concatenate([h2, ones_lanes], 1), half_up[l])
            sq = hid * hid
            t = 1.0 + jnp.tanh(hid * (2 * GELU_C + (8 * GELU_C * GELU_K) * sq))
            act = hid * t
            act_b = act.astype(bf16)
            act_scr[l] = act_b
            rest = (2.0 - t).astype(bf16)
            slope = jnp.asarray(2 * GELU_C, bf16) + jnp.asarray(24 * GELU_C * GELU_K, bf16) * sq.astype(bf16)
            gp_scr[l] = t.astype(bf16) + act_b * rest * slope
            saved.append((n1, rstd1, h1, q, k, v, mixed, rl, n2, rstd2, h2))
            x = x1 + dot(act_b, wdown[l]) + outb[l, 1:2, :]

        out_b = x.astype(bf16)
        for l in reversed(range(LAYERS)):
            n1, rstd1, h1, q, k, v, mixed, rl, n2, rstd2, h2 = saved[l]
            e2 = g.astype(bf16)
            a_small[l, 7:8, :] += row_sum(e2.astype(f32))
            du = dot_nt(e2, half_down[l]).astype(bf16) * gp_scr[l]
            dh2 = dot_nt(du, wup[l])
            a_down[l] += dot(e2.T, act_scr[l])
            both_up = dot(jnp.concatenate([h2.T, ones_rows], 0), du)
            a_up[l] += both_up[:width]
            dus = both_up[width:width + 1]
            for c in range(hidden // width):
                a_small[l, 8 + c:9 + c, :] += dus[:, c * width:(c + 1) * width]
            a_small[l, 1:2, :] += row_sum(dh2 * n2)
            a_small[l, 3:4, :] += row_sum(dh2)
            g1 = g + norm_back(dh2, n2, rstd2, gains[l, 1:2, :])
            e1 = g1.astype(bf16)
            dm = dot_nt(e1, wout[l])
            a_out[l] += dot(mixed.T, e1)
            a_small[l, 6:7, :] += row_sum(e1.astype(f32))
            dm1 = dm * rl
            dmo = -(dm1 * mixed.astype(f32))
            dm1 = dm1.astype(bf16)
            dmo = dmo.astype(bf16)
            rows_of = [slice(b * BIN, (b + 1) * BIN) for b in range(UNIT_BINS)]
            dqkv_bins = []
            for first in range(0, UNIT_BINS, BWD_GROUP):
                bins = range(first, first + BWD_GROUP)
                lhs = {b: jnp.concatenate([dm1[rows_of[b]], dmo[rows_of[b]]], 1) for b in bins}
                dm_t = {b: dm1[rows_of[b]].T for b in bins}
                q_t = {b: q[rows_of[b]].T for b in bins}
                v_t = {b: v[rows_of[b]].T for b in bins}
                dq = {b: None for b in bins}
                dv_t = {b: [] for b in bins}
                dk_t = {b: [] for b in bins}

                def d_scores(j):
                    return {b: dot(lhs[b], jnp.concatenate([pair_columns(v_t[b], j), mask_columns[j]], 0)) for b in bins}

                ahead = d_scores(0)
                for j in range(pairs):
                    top, low = 2 * j * HEAD, (2 * j + 2) * HEAD
                    z = ahead
                    if j + 1 < pairs:
                        ahead = d_scores(j + 1)
                    es = {b: e_scr[l, rows_of[b], 2 * j * BIN:(2 * j + 2) * BIN] for b in bins}
                    for b in bins:
                        pv = dot(dm_t[b][top:low], es[b])
                        dv_t[b] += [pv[:HEAD, :BIN], pv[HEAD:, BIN:]]
                    ds = {b: es[b] * z[b].astype(bf16) for b in bins}
                    for b in bins:
                        part = dot(ds[b], pair_rows(k[rows_of[b]], j))
                        dq[b] = part if dq[b] is None else dq[b] + part
                    for b in bins:
                        pk = dot(q_t[b][top:low], ds[b])
                        dk_t[b] += [pk[:HEAD, :BIN], pk[HEAD:, BIN:]]
                for b in bins:
                    dv = jnp.concatenate(dv_t[b], 0).T
                    dk = jnp.concatenate(dk_t[b], 0).T * LN2
                    dqkv_bins.append(jnp.concatenate([(dq[b] * HEAD ** -0.5).astype(bf16), dk.astype(bf16), dv.astype(bf16)], 1))
            dqkv = jnp.concatenate(dqkv_bins, 0)
            dh = dot_nt(dqkv, wqkv[l])
            both_qkv = dot(jnp.concatenate([h1.T, ones_rows], 0), dqkv)
            a_qkv[l] += both_qkv[:width]
            sums = both_qkv[width:width + 1]
            a_small[l, 4:5, :] += sums[:, :width]
            a_small[l, 5:6, :] += sums[:, 2 * width:]
            a_small[l, 0:1, :] += row_sum(dh * n1)
            a_small[l, 2:3, :] += row_sum(dh)
            g = g1 + norm_back(dh, n1, rstd1, gains[l, 0:1, :])

        grad_b = (g * factor).astype(bf16)
        s_iota = lax.broadcasted_iota(jnp.int32, (slot_rows, BIN), 0)
        p_iota = lax.broadcasted_iota(jnp.int32, (slot_rows, BIN), 1)
        both = jnp.concatenate([out_b, grad_b], 1)
        for b in range(UNIT_BINS):
            homes, picks = [], []
            for m in range(MEMBERS):
                slot = (u * UNIT_BINS + b) * MEMBERS + m
                t, o, n = mem_traj[slot], mem_off[slot], mem_len[slot]
                picks.append(jnp.where((p_iota - o == s_iota) & (s_iota < n), 1.0, 0.0).astype(bf16))
                homes.append(jnp.where(n > 0, t, trajs))
            rows = dot(jnp.concatenate(picks, 0), both[b * BIN:(b + 1) * BIN]).astype(bf16)
            for m, home in enumerate(homes):
                out[home] = rows[m * slot_rows:(m + 1) * slot_rows, :width]
                gtok[home] = rows[m * slot_rows:(m + 1) * slot_rows, width:]
        return carry

    lax.fori_loop(0, units, body, 0)

    stores = [
        pltpu.make_async_copy(out.at[pl.ds(0, trajs)], out_hbm, sems.at[0]),
        pltpu.make_async_copy(gtok.at[pl.ds(0, trajs)], gtok_hbm, sems.at[1]),
    ]
    for copy in stores:
        copy.start()
    for l in range(LAYERS):
        at = 0
        for c in range(3):
            gsum[l, at:at + width, :] = a_qkv[l, :, c * width:(c + 1) * width].astype(bf16)
            at += width
        gsum[l, at:at + width, :] = a_out[l].astype(bf16)
        at += width
        for c in range(hidden // width):
            gsum[l, at:at + width, :] = a_up[l, :, c * width:(c + 1) * width].astype(bf16)
            at += width
        for c in range(hidden // width):
            gsum[l, at:at + width, :] = a_down[l, :, c * width:(c + 1) * width].T.astype(bf16)
            at += width
        gsum[l, at:at + SMALL, :] = a_small[l].astype(bf16)
    mine = parity[0]
    half = gsum.shape[1] // 2
    stores += [
        pltpu.make_async_copy(gsum.at[l, pl.ds(i * half, half)], to, sems.at[2 + 2 * k + i])
        for k, (l, pair) in enumerate(((1 - mine, (other_a, other_b)), (mine, (mine_a, mine_b))))
        for i, to in enumerate(pair)
    ]
    for copy in stores[2:]:
        copy.start()
    for copy in stores:
        copy.wait()


def main_call(args, steps_top, parity):
    tokens, lengths, gains, shifts, wqkv, qvb, wout, outb, wup, upb, wdown, cot = args
    trajs, slot_rows, width = tokens.shape
    hidden = wup.shape[2]
    unit = BIN * UNIT_BINS
    slots = 2 * (trajs + UNIT_BINS)
    per_layer = 4 * width + 2 * hidden + SMALL
    sm = pl.BlockSpec(memory_space=pltpu.SMEM)
    hbm = pl.BlockSpec(memory_space=pl.ANY)
    sums = jax.ShapeDtypeStruct((per_layer // 2, width), bf16)
    return pl.pallas_call(
        functools.partial(main_kernel, steps_top=steps_top),
        out_shape=(
            jax.ShapeDtypeStruct(tokens.shape, bf16),
            jax.ShapeDtypeStruct(tokens.shape, bf16),
            sums,
            sums,
            sums,
            sums,
        ),
        in_specs=[sm, sm] + [hbm] * 11,
        out_specs=(hbm,) * 6,
        scratch_shapes=[
            pltpu.VMEM(tokens.shape, bf16),
            pltpu.VMEM(tokens.shape, bf16),
        ]
        + [pltpu.VMEM(a.shape, a.dtype) for a in (gains, shifts, wqkv, qvb, wout, outb, wup, upb, wdown)]
        + [
            pltpu.VMEM((trajs + 1, slot_rows, width), bf16),
            pltpu.VMEM((trajs + 1, slot_rows, width), bf16),
            pltpu.VMEM((LAYERS, per_layer, width), bf16),
            pltpu.VMEM((LAYERS, width, 3 * width), f32),
            pltpu.VMEM((LAYERS, width, width), f32),
            pltpu.VMEM((LAYERS, width, hidden), f32),
            pltpu.VMEM((LAYERS, width, hidden), f32),
            pltpu.VMEM((LAYERS, SMALL, width), f32),
            pltpu.VMEM((LAYERS, unit, width // HEAD * BIN), bf16),
            pltpu.VMEM((LAYERS, unit, hidden), bf16),
            pltpu.VMEM((LAYERS, unit, hidden), bf16),
            pltpu.VMEM((LAYERS, 2 * width, hidden), bf16),
            pltpu.VMEM((LAYERS, hidden, width), bf16),
            pltpu.SMEM((trajs,), jnp.int32),
            pltpu.SMEM((steps_top + 1,), jnp.int32),
            pltpu.SMEM((slots,), jnp.int32),
            pltpu.SMEM((slots,), jnp.int32),
            pltpu.SMEM((slots,), jnp.int32),
            pltpu.SemaphoreType.DMA((11,)),
        ],
        compiler_params=pltpu.CompilerParams(vmem_limit_bytes=56 * 1024 * 1024),
        name="layers",
    )(lengths, parity, tokens, cot, gains, shifts, wqkv, qvb, wout, outb, wup, upb, wdown)


AXES = ("dp", "group")


def finish_kernel(parity, mine_a, mine_b, other_a, other_b, gains, shifts, qkv, qvb, out, outb, up, upb, down):
    rows, width = mine_a.shape
    hidden = up.shape[2]
    for p in range(LAYERS):

        @pl.when(parity[0] == p)
        def _():
            for l in range(LAYERS):
                pieces = (mine_a, mine_b) if l == p else (other_a, other_b)

                def take(at, count):
                    found = []
                    while count > 0:
                        piece, first = divmod(at, rows)
                        now = min(count, rows - first)
                        found.append(pieces[piece][first:first + now, :].astype(f32))
                        at, count = at + now, count - now
                    return found[0] if len(found) == 1 else jnp.concatenate(found, 0)

                at = 0
                for c in range(3):
                    qkv[l, :, c * width:(c + 1) * width] = take(at, width)
                    at += width
                out[l] = take(at, width)
                at += width
                for c in range(hidden // width):
                    up[l, :, c * width:(c + 1) * width] = take(at, width)
                    at += width
                down[l] = take(at, hidden)
                at += hidden
                small = take(at, SMALL)
                gains[l] = small[0:2]
                shifts[l] = small[2:4]
                qvb[l] = small[4:6]
                outb[l] = small[6:8]
                for c in range(hidden // width):
                    upb[l:l + 1, c * width:(c + 1) * width] = small[8 + c:9 + c]


def finish_call(parity, mine, other, args):
    vm = pl.BlockSpec(memory_space=pltpu.VMEM)
    sm = pl.BlockSpec(memory_space=pltpu.SMEM)
    return pl.pallas_call(
        finish_kernel,
        out_shape=tuple(jax.ShapeDtypeStruct(a.shape, f32) for a in args[2:11]),
        in_specs=[sm] + [vm] * 4,
        out_specs=(vm,) * 9,
        compiler_params=pltpu.CompilerParams(vmem_limit_bytes=16 * 1024 * 1024),
        name="finish",
    )(parity, *mine, *other)


def exchange(x, bits, devices):
    return lax.ppermute(x, AXES, [(i, i ^ bits[i % 2]) for i in range(devices)])


def added(a, b):
    return (a.astype(f32) + b.astype(f32)).astype(bf16)


def all_sum(mine, other, index, devices):
    bits = [1 << i for i in range(1, devices.bit_length() - 1)]
    crossed = list(bits)
    for i in range(0, len(bits) - 1, 2):
        crossed[i], crossed[i + 1] = bits[i + 1], bits[i]
    steps = list(zip(bits, crossed))
    order = []
    for i in range(0, len(steps), 4):
        some = steps[i:i + 4]
        order += some[0::2] + some[1::2]
    turned = list(order)
    for i in range(0, len(order) - 1, 2):
        turned[i], turned[i + 1] = order[i + 1], order[i]
    orders = [order, turned]
    parts = [added(m, exchange(o, (1, 1), devices)) for m, o in zip(mine, other)]
    lows = [(index // jnp.where(index % 2 == 0, order[0][0], order[0][1])) % 2 == 0 for order in orders]
    half = parts[0].shape[0] // 2
    kept = [jnp.where(low, p[:half], p[half:]) for p, low in zip(parts, lows)]
    sent = [jnp.where(low, p[half:], p[:half]) for p, low in zip(parts, lows)]
    for step in range(len(steps)):
        got = [exchange(p, order[step], devices) for p, order in zip(sent, orders)]
        kept = [added(p, q) for p, q in zip(kept, got)]
        sent = kept
    got = [exchange(p, order[0], devices) for p, order in zip(kept, orders)]
    parts = [
        jnp.where(low, jnp.concatenate([p, q]), jnp.concatenate([q, p]))
        for p, q, low in zip(kept, got, lows)
    ]
    return parts, [exchange(p, (1, 1), devices) for p in parts]


def solution(mesh):
    mesh_shape = dict(mesh.shape)
    devices = mesh_shape["dp"] * mesh_shape["group"]

    def per_device(*args):
        index = lax.axis_index("dp") * mesh_shape["group"] + lax.axis_index("group")
        parity = (index % 2).astype(jnp.int32).reshape(1)
        output, grad_tokens, mine_a, mine_b, other_a, other_b = main_call(args, STEPS, parity)
        mine, other = all_sum((mine_a, mine_b), (other_a, other_b), index, devices)
        return (output, grad_tokens) + tuple(finish_call(parity, mine, other, args))

    rows = P(AXES, None, None)
    return jax.shard_map(
        per_device,
        mesh=mesh,
        in_specs=(rows, P(AXES)) + (P(),) * 9 + (rows,),
        out_specs=(rows, rows) + (P(),) * 9,
        check_vma=False,
    )
```

```python
import functools
import jax
import jax.numpy as jnp
from jax import lax
from jax.sharding import PartitionSpec as P
from jax.experimental import pallas as pl
from jax.experimental.pallas import tpu as pltpu

STEPS = 30
HEAD = 16
LAYERS = 2
BIN = 128
SMALL = 64
FWD_GROUP = 1
BWD_GROUP = 4
MEMBERS = 2
UNIT_BINS = 8
eps = 1e-05
dead_score = -1e30
LOG2E = 1.4426950408889634
LN2 = 0.6931471805599453
GELU_C = 0.7978845608
GELU_K = 0.044715
bf16 = jnp.bfloat16
f32 = jnp.float32


def dot(a, b):
    return lax.dot_general(a, b, (((1,), (0,)), ((), ())), preferred_element_type=f32)


def dot_nt(a, b):
    return lax.dot_general(a, b, (((1,), (1,)), ((), ())), preferred_element_type=f32)


def plan(lengths, order, count, mem_traj, mem_off, mem_len, steps_top):
    trajs = lengths.shape[0]
    pairs = trajs // 2

    def clear(i, c):
        count[i] = 0
        return c

    lax.fori_loop(0, steps_top + 1, clear, 0, unroll=True)

    def tally(t, c):
        s = lengths[t] // 3
        count[s] = count[s] + 1
        return c

    lax.fori_loop(0, trajs, tally, 0, unroll=4)

    def prefix(i, total):
        s = steps_top - i
        n = count[s]
        count[s] = total
        return total + n

    lax.fori_loop(0, steps_top + 1, prefix, 0, unroll=True)

    def rank(t, c):
        s = lengths[t] // 3
        p = count[s]
        order[p] = t
        count[s] = p + 1
        return c

    lax.fori_loop(0, trajs, rank, 0, unroll=4)

    def member(slot, t, offset, length):
        mem_traj[slot] = t
        mem_off[slot] = offset
        mem_len[slot] = length

    def pair(p, nbins):
        long, short = order[p], order[trajs - 1 - p]
        length, length_two = lengths[long], lengths[short]
        fits = length + length_two <= BIN
        member(2 * p, long, 0, length)
        member(2 * p + 1, short, length, jnp.where(fits, length_two, 0))
        member(2 * nbins, short, 0, length_two)
        member(2 * nbins + 1, short, length_two, 0)
        return nbins + jnp.where(fits, 0, 1)

    nbins = lax.fori_loop(0, pairs, pair, pairs)
    units = (nbins + UNIT_BINS - 1) // UNIT_BINS

    def pad(i, c):
        member(i, 0, BIN, 0)
        return c

    lax.fori_loop(2 * nbins, 2 * UNIT_BINS * units, pad, 0)
    return units


def norm_parts(x):
    c = x - jnp.mean(x, -1, keepdims=True)
    rstd = lax.rsqrt(jnp.mean(c * c, -1, keepdims=True) + eps)
    return c * rstd, rstd


def norm_back(dy, normed, rstd, gain):
    dg = dy * gain
    return (dg - jnp.mean(dg, -1, keepdims=True) - normed * jnp.mean(dg * normed, -1, keepdims=True)) * rstd


def head_masks(width):
    lane = lax.broadcasted_iota(jnp.int32, (1, width), 1) // HEAD
    return [jnp.where(lane == h, 1.0, 0.0).astype(bf16) for h in range(width // HEAD)]


def row_sum(x):
    return jnp.sum(x, 0, keepdims=True)


def main_kernel(
    lengths, parity, tok_hbm, cot_hbm, gains_hbm, shifts_hbm, wqkv_hbm, qvb_hbm, wout_hbm, outb_hbm, wup_hbm, upb_hbm, wdown_hbm,
    out_hbm, gtok_hbm, mine_a, mine_b, other_a, other_b,
    tok, cot, gains, shifts, wqkv, qvb, wout, outb, wup, upb, wdown, out, gtok, gsum,
    a_qkv, a_out, a_up, a_down, a_small, e_scr, act_scr, gp_scr, half_up, half_down,
    order, count, mem_traj, mem_off, mem_len, sems,
    *, steps_top,
):
    trajs, slot_rows, width = tok.shape
    hidden = wup.shape[2]
    heads = width // HEAD
    pairs = heads // 2
    unit = BIN * UNIT_BINS
    sources = (tok_hbm, cot_hbm, gains_hbm, shifts_hbm, wqkv_hbm, qvb_hbm, wout_hbm, outb_hbm, wup_hbm, upb_hbm, wdown_hbm)
    targets = (tok, cot, gains, shifts, wqkv, qvb, wout, outb, wup, upb, wdown)
    loads = [pltpu.make_async_copy(a, b, sems.at[i]) for i, (a, b) in enumerate(zip(sources, targets))]
    for copy in loads:
        copy.start()
    for ref in (a_qkv, a_out, a_up, a_down, a_small):
        ref[...] = jnp.zeros_like(ref)
    units = plan(lengths, order, count, mem_traj, mem_off, mem_len, steps_top)
    for copy in loads:
        copy.wait()

    at = lax.broadcasted_iota(jnp.int32, (width, hidden), 0)
    for l in range(LAYERS):
        bias = 0.5 * upb[l:l + 1, :]
        high = bias.astype(bf16).astype(f32)
        half_up[l, :width, :] = wup[l] * jnp.asarray(0.5, bf16)
        half_up[l, width:, :] = jnp.where(at == 0, high, jnp.where(at == 1, bias - high, 0.0)).astype(bf16)
        half_down[l] = wdown[l] * jnp.asarray(0.5, bf16)

    masks = head_masks(width)
    mask_pairs = [
        jnp.concatenate([jnp.broadcast_to(masks[2 * j], (BIN, width)), jnp.broadcast_to(masks[2 * j + 1], (BIN, width))], 0)
        for j in range(pairs)
    ]

    def pair_rows(x, j):
        return jnp.concatenate([x * masks[2 * j], x * masks[2 * j + 1]], 0)

    blank = jnp.zeros((HEAD, BIN), bf16)
    ones = jnp.ones((HEAD, BIN), bf16)

    def pair_columns(xt, j):
        lo, mid, hi = 2 * j * HEAD, (2 * j + 1) * HEAD, (2 * j + 2) * HEAD
        parts = [
            jnp.concatenate([xt[lo:mid], blank], 1),
            jnp.concatenate([blank, xt[mid:hi]], 1),
        ]
        if j > 0:
            parts = [jnp.zeros((lo, 2 * BIN), bf16)] + parts
        if hi < width:
            parts = parts + [jnp.zeros((width - hi, 2 * BIN), bf16)]
        return jnp.concatenate(parts, 0)

    ones_t = jnp.ones((width, BIN), bf16)
    mask_columns = [pair_columns(ones_t, j) for j in range(pairs)]

    lane = lax.broadcasted_iota(jnp.int32, (unit, width), 1)
    ones_rows = jnp.ones((16, unit), bf16)
    ones_lanes = jnp.where(lane < 2, 1.0, 0.0).astype(bf16)

    def body(u, carry):
        q_iota = lax.broadcasted_iota(jnp.int32, (BIN, BIN), 0)
        k_iota = lax.broadcasted_iota(jnp.int32, (BIN, BIN), 1)
        toks, cots, biases = [], [], []
        for b in range(UNIT_BINS):
            picks, rows_in = [], []
            start = jnp.zeros((BIN, BIN), jnp.int32)
            for m in range(MEMBERS):
                slot = (u * UNIT_BINS + b) * MEMBERS + m
                t, o, n = mem_traj[slot], mem_off[slot], mem_len[slot]
                picks.append(jnp.where((q_iota - o == k_iota) & (k_iota < n), 1.0, 0.0).astype(bf16))
                rows_in += [jnp.concatenate([tok[t], cot[t]], axis=1), jnp.zeros((BIN - slot_rows, 2 * width), bf16)]
                start = jnp.where(q_iota >= o + n, o + n, start)
            x = dot(jnp.concatenate(picks, 1), jnp.concatenate(rows_in, 0))
            toks.append(x[:, :width])
            cots.append(x[:, width:])
            biases.append(jnp.where((k_iota <= q_iota) & (k_iota >= start), 0.0, dead_score))
        x = jnp.concatenate(toks, 0)
        g = jnp.concatenate(cots, 0)
        row = lax.broadcasted_iota(jnp.int32, (unit, 1), 0) % BIN
        factor = jnp.where(row % 3 == 0, 0.5, 1.0)
        x = x * factor

        saved = []
        for l in range(LAYERS):
            n1, rstd1 = norm_parts(x)
            h1 = (n1 * gains[l, 0:1, :] + shifts[l, 0:1, :]).astype(bf16)
            joint = dot(h1, wqkv[l])
            q = ((joint[:, :width] + qvb[l, 0:1, :]) * (LOG2E * HEAD ** -0.5)).astype(bf16)
            k = joint[:, width:2 * width].astype(bf16)
            v = (joint[:, 2 * width:] + qvb[l, 1:2, :]).astype(bf16)
            rows_of = [slice(b * BIN, (b + 1) * BIN) for b in range(UNIT_BINS)]
            mixed_bins, rl_bins = [], []
            for first in range(0, UNIT_BINS, FWD_GROUP):
                bins = range(first, first + FWD_GROUP)
                acc = {b: None for b in bins}

                def scores(j):
                    return {b: dot_nt(q[rows_of[b]], pair_rows(k[rows_of[b]], j)) for b in bins}

                ahead = scores(0)
                for j in range(pairs):
                    s = ahead
                    if j + 1 < pairs:
                        ahead = scores(j + 1)
                    es = {}
                    for b in bins:
                        halves = []
                        for half in range(2):
                            sh = s[b][:, half * BIN:(half + 1) * BIN] + biases[b]
                            halves.append(jnp.exp2(sh - jnp.max(sh, -1, keepdims=True)).astype(bf16))
                        es[b] = jnp.concatenate(halves, 1)
                        e_scr[l, rows_of[b], 2 * j * BIN:(2 * j + 2) * BIN] = es[b]
                    for b in bins:
                        part = dot(es[b], jnp.concatenate([pair_rows(v[rows_of[b]], j), mask_pairs[j]], 1))
                        acc[b] = part if acc[b] is None else acc[b] + part
                for b in bins:
                    rl = 1.0 / acc[b][:, width:]
                    mixed_bins.append((acc[b][:, :width] * rl).astype(bf16))
                    rl_bins.append(rl)
            mixed = jnp.concatenate(mixed_bins, 0)
            rl = jnp.concatenate(rl_bins, 0)
            x1 = x + dot(mixed, wout[l]) + outb[l, 0:1, :]
            n2, rstd2 = norm_parts(x1)
            h2 = (n2 * gains[l, 1:2, :] + shifts[l, 1:2, :]).astype(bf16)
            hid = dot(jnp.concatenate([h2, ones_lanes], 1), half_up[l])
            sq = hid * hid
            t = 1.0 + jnp.tanh(hid * (2 * GELU_C + (8 * GELU_C * GELU_K) * sq))
            act = hid * t
            act_b = act.astype(bf16)
            act_scr[l] = act_b
            rest = (2.0 - t).astype(bf16)
            slope = jnp.asarray(2 * GELU_C, bf16) + jnp.asarray(24 * GELU_C * GELU_K, bf16) * sq.astype(bf16)
            gp_scr[l] = t.astype(bf16) + act_b * rest * slope
            saved.append((n1, rstd1, h1, q, k, v, mixed, rl, n2, rstd2, h2))
            x = x1 + dot(act_b, wdown[l]) + outb[l, 1:2, :]

        out_b = x.astype(bf16)
        for l in reversed(range(LAYERS)):
            n1, rstd1, h1, q, k, v, mixed, rl, n2, rstd2, h2 = saved[l]
            e2 = g.astype(bf16)
            a_small[l, 7:8, :] += row_sum(e2.astype(f32))
            du = dot_nt(e2, half_down[l]).astype(bf16) * gp_scr[l]
            dh2 = dot_nt(du, wup[l])
            a_down[l] += dot(e2.T, act_scr[l])
            both_up = dot(jnp.concatenate([h2.T, ones_rows], 0), du)
            a_up[l] += both_up[:width]
            dus = both_up[width:width + 1]
            for c in range(hidden // width):
                a_small[l, 8 + c:9 + c, :] += dus[:, c * width:(c + 1) * width]
            a_small[l, 1:2, :] += row_sum(dh2 * n2)
            a_small[l, 3:4, :] += row_sum(dh2)
            g1 = g + norm_back(dh2, n2, rstd2, gains[l, 1:2, :])
            e1 = g1.astype(bf16)
            dm = dot_nt(e1, wout[l])
            a_out[l] += dot(mixed.T, e1)
            a_small[l, 6:7, :] += row_sum(e1.astype(f32))
            dm1 = dm * rl
            dmo = -(dm1 * mixed.astype(f32))
            dm1 = dm1.astype(bf16)
            dmo = dmo.astype(bf16)
            rows_of = [slice(b * BIN, (b + 1) * BIN) for b in range(UNIT_BINS)]
            dqkv_bins = []
            for first in range(0, UNIT_BINS, BWD_GROUP):
                bins = range(first, first + BWD_GROUP)
                lhs = {b: jnp.concatenate([dm1[rows_of[b]], dmo[rows_of[b]]], 1) for b in bins}
                dm_t = {b: dm1[rows_of[b]].T for b in bins}
                q_t = {b: q[rows_of[b]].T for b in bins}
                v_t = {b: v[rows_of[b]].T for b in bins}
                dq = {b: None for b in bins}
                dv_t = {b: [] for b in bins}
                dk_t = {b: [] for b in bins}

                def d_scores(j):
                    return {b: dot(lhs[b], jnp.concatenate([pair_columns(v_t[b], j), mask_columns[j]], 0)) for b in bins}

                ahead = d_scores(0)
                for j in range(pairs):
                    top, low = 2 * j * HEAD, (2 * j + 2) * HEAD
                    z = ahead
                    if j + 1 < pairs:
                        ahead = d_scores(j + 1)
                    es = {b: e_scr[l, rows_of[b], 2 * j * BIN:(2 * j + 2) * BIN] for b in bins}
                    for b in bins:
                        pv = dot(dm_t[b][top:low], es[b])
                        dv_t[b] += [pv[:HEAD, :BIN], pv[HEAD:, BIN:]]
                    ds = {b: es[b] * z[b].astype(bf16) for b in bins}
                    for b in bins:
                        part = dot(ds[b], pair_rows(k[rows_of[b]], j))
                        dq[b] = part if dq[b] is None else dq[b] + part
                    for b in bins:
                        pk = dot(q_t[b][top:low], ds[b])
                        dk_t[b] += [pk[:HEAD, :BIN], pk[HEAD:, BIN:]]
                for b in bins:
                    dv = jnp.concatenate(dv_t[b], 0).T
                    dk = jnp.concatenate(dk_t[b], 0).T * LN2
                    dqkv_bins.append(jnp.concatenate([(dq[b] * HEAD ** -0.5).astype(bf16), dk.astype(bf16), dv.astype(bf16)], 1))
            dqkv = jnp.concatenate(dqkv_bins, 0)
            dh = dot_nt(dqkv, wqkv[l])
            both_qkv = dot(jnp.concatenate([h1.T, ones_rows], 0), dqkv)
            a_qkv[l] += both_qkv[:width]
            sums = both_qkv[width:width + 1]
            a_small[l, 4:5, :] += sums[:, :width]
            a_small[l, 5:6, :] += sums[:, 2 * width:]
            a_small[l, 0:1, :] += row_sum(dh * n1)
            a_small[l, 2:3, :] += row_sum(dh)
            g = g1 + norm_back(dh, n1, rstd1, gains[l, 0:1, :])

        grad_b = (g * factor).astype(bf16)
        s_iota = lax.broadcasted_iota(jnp.int32, (slot_rows, BIN), 0)
        p_iota = lax.broadcasted_iota(jnp.int32, (slot_rows, BIN), 1)
        both = jnp.concatenate([out_b, grad_b], 1)
        for b in range(UNIT_BINS):
            homes, picks = [], []
            for m in range(MEMBERS):
                slot = (u * UNIT_BINS + b) * MEMBERS + m
                t, o, n = mem_traj[slot], mem_off[slot], mem_len[slot]
                picks.append(jnp.where((p_iota - o == s_iota) & (s_iota < n), 1.0, 0.0).astype(bf16))
                homes.append(jnp.where(n > 0, t, trajs))
            rows = dot(jnp.concatenate(picks, 0), both[b * BIN:(b + 1) * BIN]).astype(bf16)
            for m, home in enumerate(homes):
                out[home] = rows[m * slot_rows:(m + 1) * slot_rows, :width]
                gtok[home] = rows[m * slot_rows:(m + 1) * slot_rows, width:]
        return carry

    lax.fori_loop(0, units, body, 0)

    stores = [
        pltpu.make_async_copy(out.at[pl.ds(0, trajs)], out_hbm, sems.at[0]),
        pltpu.make_async_copy(gtok.at[pl.ds(0, trajs)], gtok_hbm, sems.at[1]),
    ]
    for copy in stores:
        copy.start()
    for l in range(LAYERS):
        at = 0
        for c in range(3):
            gsum[l, at:at + width, :] = a_qkv[l, :, c * width:(c + 1) * width].astype(bf16)
            at += width
        gsum[l, at:at + width, :] = a_out[l].astype(bf16)
        at += width
        for c in range(hidden // width):
            gsum[l, at:at + width, :] = a_up[l, :, c * width:(c + 1) * width].astype(bf16)
            at += width
        for c in range(hidden // width):
            gsum[l, at:at + width, :] = a_down[l, :, c * width:(c + 1) * width].T.astype(bf16)
            at += width
        gsum[l, at:at + SMALL, :] = a_small[l].astype(bf16)
    mine = parity[0]
    half = gsum.shape[1] // 2
    stores += [
        pltpu.make_async_copy(gsum.at[l, pl.ds(i * half, half)], to, sems.at[2 + 2 * k + i])
        for k, (l, pair) in enumerate(((1 - mine, (other_a, other_b)), (mine, (mine_a, mine_b))))
        for i, to in enumerate(pair)
    ]
    for copy in stores[2:]:
        copy.start()
    for copy in stores:
        copy.wait()


def main_call(args, steps_top, parity):
    tokens, lengths, gains, shifts, wqkv, qvb, wout, outb, wup, upb, wdown, cot = args
    trajs, slot_rows, width = tokens.shape
    hidden = wup.shape[2]
    unit = BIN * UNIT_BINS
    slots = 2 * (trajs + UNIT_BINS)
    per_layer = 4 * width + 2 * hidden + SMALL
    sm = pl.BlockSpec(memory_space=pltpu.SMEM)
    hbm = pl.BlockSpec(memory_space=pl.ANY)
    sums = jax.ShapeDtypeStruct((per_layer // 2, width), bf16)
    return pl.pallas_call(
        functools.partial(main_kernel, steps_top=steps_top),
        out_shape=(
            jax.ShapeDtypeStruct(tokens.shape, bf16),
            jax.ShapeDtypeStruct(tokens.shape, bf16),
            sums,
            sums,
            sums,
            sums,
        ),
        in_specs=[sm, sm] + [hbm] * 11,
        out_specs=(hbm,) * 6,
        scratch_shapes=[
            pltpu.VMEM(tokens.shape, bf16),
            pltpu.VMEM(tokens.shape, bf16),
        ]
        + [pltpu.VMEM(a.shape, a.dtype) for a in (gains, shifts, wqkv, qvb, wout, outb, wup, upb, wdown)]
        + [
            pltpu.VMEM((trajs + 1, slot_rows, width), bf16),
            pltpu.VMEM((trajs + 1, slot_rows, width), bf16),
            pltpu.VMEM((LAYERS, per_layer, width), bf16),
            pltpu.VMEM((LAYERS, width, 3 * width), f32),
            pltpu.VMEM((LAYERS, width, width), f32),
            pltpu.VMEM((LAYERS, width, hidden), f32),
            pltpu.VMEM((LAYERS, width, hidden), f32),
            pltpu.VMEM((LAYERS, SMALL, width), f32),
            pltpu.VMEM((LAYERS, unit, width // HEAD * BIN), bf16),
            pltpu.VMEM((LAYERS, unit, hidden), bf16),
            pltpu.VMEM((LAYERS, unit, hidden), bf16),
            pltpu.VMEM((LAYERS, 2 * width, hidden), bf16),
            pltpu.VMEM((LAYERS, hidden, width), bf16),
            pltpu.SMEM((trajs,), jnp.int32),
            pltpu.SMEM((steps_top + 1,), jnp.int32),
            pltpu.SMEM((slots,), jnp.int32),
            pltpu.SMEM((slots,), jnp.int32),
            pltpu.SMEM((slots,), jnp.int32),
            pltpu.SemaphoreType.DMA((11,)),
        ],
        compiler_params=pltpu.CompilerParams(vmem_limit_bytes=56 * 1024 * 1024),
        name="layers",
    )(lengths, parity, tokens, cot, gains, shifts, wqkv, qvb, wout, outb, wup, upb, wdown)


AXES = ("dp", "group")


def finish_kernel(parity, mine_a, mine_b, other_a, other_b, gains, shifts, qkv, qvb, out, outb, up, upb, down):
    rows, width = mine_a.shape
    hidden = up.shape[2]
    for p in range(LAYERS):

        @pl.when(parity[0] == p)
        def _():
            for l in range(LAYERS):
                pieces = (mine_a, mine_b) if l == p else (other_a, other_b)

                def take(at, count):
                    found = []
                    while count > 0:
                        piece, first = divmod(at, rows)
                        now = min(count, rows - first)
                        found.append(pieces[piece][first:first + now, :].astype(f32))
                        at, count = at + now, count - now
                    return found[0] if len(found) == 1 else jnp.concatenate(found, 0)

                at = 0
                for c in range(3):
                    qkv[l, :, c * width:(c + 1) * width] = take(at, width)
                    at += width
                out[l] = take(at, width)
                at += width
                for c in range(hidden // width):
                    up[l, :, c * width:(c + 1) * width] = take(at, width)
                    at += width
                down[l] = take(at, hidden)
                at += hidden
                small = take(at, SMALL)
                gains[l] = small[0:2]
                shifts[l] = small[2:4]
                qvb[l] = small[4:6]
                outb[l] = small[6:8]
                for c in range(hidden // width):
                    upb[l:l + 1, c * width:(c + 1) * width] = small[8 + c:9 + c]


def finish_call(parity, mine, other, args):
    vm = pl.BlockSpec(memory_space=pltpu.VMEM)
    sm = pl.BlockSpec(memory_space=pltpu.SMEM)
    return pl.pallas_call(
        finish_kernel,
        out_shape=tuple(jax.ShapeDtypeStruct(a.shape, f32) for a in args[2:11]),
        in_specs=[sm] + [vm] * 4,
        out_specs=(vm,) * 9,
        compiler_params=pltpu.CompilerParams(vmem_limit_bytes=16 * 1024 * 1024),
        name="finish",
    )(parity, *mine, *other)


def exchange(x, bits, devices):
    return lax.ppermute(x, AXES, [(i, i ^ bits[i % 2]) for i in range(devices)])


def added(a, b):
    return (a.astype(f32) + b.astype(f32)).astype(bf16)


def picked(pieces, at):
    first, low = (at // 2) % 2 == 0, at % 2 == 0
    return jnp.where(first, jnp.where(low, pieces[0], pieces[1]), jnp.where(low, pieces[2], pieces[3]))


def all_sum(mine, other, index, devices):
    parts = [added(m, exchange(o, (1, 1), devices)) for m, o in zip(mine, other)]
    half = parts[0].shape[0] // 2
    quarters = [parts[0][:half], parts[0][half:], parts[1][:half], parts[1][half:]]
    bits = [1 << i for i in range(1, devices.bit_length() - 1)]
    rest = bits[2:]
    crossed = list(rest)
    for i in range(0, len(rest) - 1, 2):
        crossed[i], crossed[i + 1] = rest[i + 1], rest[i]
    turns = {m: m * bits[0] for m in (1, 2, 3)}
    place = (index // bits[0]) % 4
    got = [exchange(picked(quarters, place ^ m), (bit, bit), devices) for m, bit in turns.items()]
    total = picked(quarters, place).astype(f32)
    for piece in got:
        total = total + piece.astype(f32)
    total = total.astype(bf16)
    for step in zip(rest, crossed):
        total = added(total, exchange(total, step, devices))
    have = {0: total}
    for m, bit in turns.items():
        have[m] = exchange(total, (bit, bit), devices)
    pieces = [have[m] for m in range(4)]
    parts = [jnp.concatenate([picked(pieces, place ^ j), picked(pieces, place ^ (j + 1))]) for j in (0, 2)]
    return parts, [exchange(p, (1, 1), devices) for p in parts]


def solution(mesh):
    mesh_shape = dict(mesh.shape)
    devices = mesh_shape["dp"] * mesh_shape["group"]

    def per_device(*args):
        index = lax.axis_index("dp") * mesh_shape["group"] + lax.axis_index("group")
        parity = (index % 2).astype(jnp.int32).reshape(1)
        output, grad_tokens, mine_a, mine_b, other_a, other_b = main_call(args, STEPS, parity)
        mine, other = all_sum((mine_a, mine_b), (other_a, other_b), index, devices)
        return (output, grad_tokens) + tuple(finish_call(parity, mine, other, args))

    rows = P(AXES, None, None)
    return jax.shard_map(
        per_device,
        mesh=mesh,
        in_specs=(rows, P(AXES)) + (P(),) * 9 + (rows,),
        out_specs=(rows, rows) + (P(),) * 9,
        check_vma=False,
    )
```

```python
import functools
import jax
import jax.numpy as jnp
from jax import lax
from jax.sharding import PartitionSpec as P
from jax.experimental import pallas as pl
from jax.experimental.pallas import tpu as pltpu

STEPS = 30
HEAD = 16
LAYERS = 2
BIN = 128
SMALL = 32
FWD_GROUP = 1
BWD_GROUP = 4
MEMBERS = 2
UNIT_BINS = 8
eps = 1e-05
dead_score = -1e30
LOG2E = 1.4426950408889634
LN2 = 0.6931471805599453
GELU_C = 0.7978845608
GELU_K = 0.044715
bf16 = jnp.bfloat16
f32 = jnp.float32


def dot(a, b):
    return lax.dot_general(a, b, (((1,), (0,)), ((), ())), preferred_element_type=f32)


def dot_nt(a, b):
    return lax.dot_general(a, b, (((1,), (1,)), ((), ())), preferred_element_type=f32)


def plan(lengths, order, count, mem_traj, mem_off, mem_len, steps_top):
    trajs = lengths.shape[0]
    pairs = trajs // 2

    def clear(i, c):
        count[i] = 0
        return c

    lax.fori_loop(0, steps_top + 1, clear, 0, unroll=True)

    def tally(t, c):
        s = lengths[t] // 3
        count[s] = count[s] + 1
        return c

    lax.fori_loop(0, trajs, tally, 0, unroll=4)

    def prefix(i, total):
        s = steps_top - i
        n = count[s]
        count[s] = total
        return total + n

    lax.fori_loop(0, steps_top + 1, prefix, 0, unroll=True)

    def rank(t, c):
        s = lengths[t] // 3
        p = count[s]
        order[p] = t
        count[s] = p + 1
        return c

    lax.fori_loop(0, trajs, rank, 0, unroll=4)

    def member(slot, t, offset, length):
        mem_traj[slot] = t
        mem_off[slot] = offset
        mem_len[slot] = length

    def pair(p, nbins):
        long, short = order[p], order[trajs - 1 - p]
        length, length_two = lengths[long], lengths[short]
        fits = length + length_two <= BIN
        member(2 * p, long, 0, length)
        member(2 * p + 1, short, length, jnp.where(fits, length_two, 0))
        member(2 * nbins, short, 0, length_two)
        member(2 * nbins + 1, short, length_two, 0)
        return nbins + jnp.where(fits, 0, 1)

    nbins = lax.fori_loop(0, pairs, pair, pairs)
    units = (nbins + UNIT_BINS - 1) // UNIT_BINS

    def pad(i, c):
        member(i, 0, BIN, 0)
        return c

    lax.fori_loop(2 * nbins, 2 * UNIT_BINS * units, pad, 0)
    return units


def norm_parts(x):
    c = x - jnp.mean(x, -1, keepdims=True)
    rstd = lax.rsqrt(jnp.mean(c * c, -1, keepdims=True) + eps)
    return c * rstd, rstd


def norm_back(dy, normed, rstd, gain):
    dg = dy * gain
    return (dg - jnp.mean(dg, -1, keepdims=True) - normed * jnp.mean(dg * normed, -1, keepdims=True)) * rstd


def head_masks(width):
    lane = lax.broadcasted_iota(jnp.int32, (1, width), 1) // HEAD
    return [jnp.where(lane == h, 1.0, 0.0).astype(bf16) for h in range(width // HEAD)]


def row_sum(x):
    return jnp.sum(x, 0, keepdims=True)


def main_kernel(
    lengths, parity, tok_hbm, cot_hbm, gains_hbm, shifts_hbm, wqkv_hbm, qvb_hbm, wout_hbm, outb_hbm, wup_hbm, upb_hbm, wdown_hbm,
    out_hbm, gtok_hbm, mine_a, mine_b, other_a, other_b,
    tok, cot, gains, shifts, wqkv, qvb, wout, outb, wup, upb, wdown, out, gtok, gsum,
    a_qkv, a_out, a_up, a_down, a_small, e_scr, act_scr, gp_scr, half_up, half_down,
    order, count, mem_traj, mem_off, mem_len, sems,
    *, steps_top,
):
    trajs, slot_rows, width = tok.shape
    hidden = wup.shape[2]
    heads = width // HEAD
    pairs = heads // 2
    unit = BIN * UNIT_BINS
    sources = (tok_hbm, cot_hbm, gains_hbm, shifts_hbm, wqkv_hbm, qvb_hbm, wout_hbm, outb_hbm, wup_hbm, upb_hbm, wdown_hbm)
    targets = (tok, cot, gains, shifts, wqkv, qvb, wout, outb, wup, upb, wdown)
    loads = [pltpu.make_async_copy(a, b, sems.at[i]) for i, (a, b) in enumerate(zip(sources, targets))]
    for copy in loads:
        copy.start()
    for ref in (a_qkv, a_out, a_up, a_down, a_small):
        ref[...] = jnp.zeros_like(ref)
    units = plan(lengths, order, count, mem_traj, mem_off, mem_len, steps_top)
    for copy in loads:
        copy.wait()

    at = lax.broadcasted_iota(jnp.int32, (width, hidden), 0)
    for l in range(LAYERS):
        bias = 0.5 * upb[l:l + 1, :]
        high = bias.astype(bf16).astype(f32)
        half_up[l, :width, :] = wup[l] * jnp.asarray(0.5, bf16)
        half_up[l, width:, :] = jnp.where(at == 0, high, jnp.where(at == 1, bias - high, 0.0)).astype(bf16)
        half_down[l] = wdown[l] * jnp.asarray(0.5, bf16)

    masks = head_masks(width)
    mask_pairs = [
        jnp.concatenate([jnp.broadcast_to(masks[2 * j], (BIN, width)), jnp.broadcast_to(masks[2 * j + 1], (BIN, width))], 0)
        for j in range(pairs)
    ]

    def pair_rows(x, j):
        return jnp.concatenate([x * masks[2 * j], x * masks[2 * j + 1]], 0)

    blank = jnp.zeros((HEAD, BIN), bf16)
    ones = jnp.ones((HEAD, BIN), bf16)

    def pair_columns(xt, j):
        lo, mid, hi = 2 * j * HEAD, (2 * j + 1) * HEAD, (2 * j + 2) * HEAD
        parts = [
            jnp.concatenate([xt[lo:mid], blank], 1),
            jnp.concatenate([blank, xt[mid:hi]], 1),
        ]
        if j > 0:
            parts = [jnp.zeros((lo, 2 * BIN), bf16)] + parts
        if hi < width:
            parts = parts + [jnp.zeros((width - hi, 2 * BIN), bf16)]
        return jnp.concatenate(parts, 0)

    ones_t = jnp.ones((width, BIN), bf16)
    mask_columns = [pair_columns(ones_t, j) for j in range(pairs)]

    lane = lax.broadcasted_iota(jnp.int32, (unit, width), 1)
    ones_rows = jnp.ones((16, unit), bf16)
    ones_lanes = jnp.where(lane < 2, 1.0, 0.0).astype(bf16)

    def body(u, carry):
        q_iota = lax.broadcasted_iota(jnp.int32, (BIN, BIN), 0)
        k_iota = lax.broadcasted_iota(jnp.int32, (BIN, BIN), 1)
        toks, cots, biases = [], [], []
        for b in range(UNIT_BINS):
            picks, rows_in = [], []
            start = jnp.zeros((BIN, BIN), jnp.int32)
            for m in range(MEMBERS):
                slot = (u * UNIT_BINS + b) * MEMBERS + m
                t, o, n = mem_traj[slot], mem_off[slot], mem_len[slot]
                picks.append(jnp.where((q_iota - o == k_iota) & (k_iota < n), 1.0, 0.0).astype(bf16))
                rows_in += [jnp.concatenate([tok[t], cot[t]], axis=1), jnp.zeros((BIN - slot_rows, 2 * width), bf16)]
                start = jnp.where(q_iota >= o + n, o + n, start)
            x = dot(jnp.concatenate(picks, 1), jnp.concatenate(rows_in, 0))
            toks.append(x[:, :width])
            cots.append(x[:, width:])
            biases.append(jnp.where((k_iota <= q_iota) & (k_iota >= start), 0.0, dead_score))
        x = jnp.concatenate(toks, 0)
        g = jnp.concatenate(cots, 0)
        row = lax.broadcasted_iota(jnp.int32, (unit, 1), 0) % BIN
        factor = jnp.where(row % 3 == 0, 0.5, 1.0)
        x = x * factor

        saved = []
        for l in range(LAYERS):
            n1, rstd1 = norm_parts(x)
            h1 = (n1 * gains[l, 0:1, :] + shifts[l, 0:1, :]).astype(bf16)
            joint = dot(h1, wqkv[l])
            q = ((joint[:, :width] + qvb[l, 0:1, :]) * (LOG2E * HEAD ** -0.5)).astype(bf16)
            k = joint[:, width:2 * width].astype(bf16)
            v = (joint[:, 2 * width:] + qvb[l, 1:2, :]).astype(bf16)
            rows_of = [slice(b * BIN, (b + 1) * BIN) for b in range(UNIT_BINS)]
            mixed_bins, rl_bins = [], []
            for first in range(0, UNIT_BINS, FWD_GROUP):
                bins = range(first, first + FWD_GROUP)
                acc = {b: None for b in bins}

                def scores(j):
                    return {b: dot_nt(q[rows_of[b]], pair_rows(k[rows_of[b]], j)) for b in bins}

                ahead = scores(0)
                for j in range(pairs):
                    s = ahead
                    if j + 1 < pairs:
                        ahead = scores(j + 1)
                    es = {}
                    for b in bins:
                        halves = []
                        for half in range(2):
                            sh = s[b][:, half * BIN:(half + 1) * BIN] + biases[b]
                            halves.append(jnp.exp2(sh - jnp.max(sh, -1, keepdims=True)).astype(bf16))
                        es[b] = jnp.concatenate(halves, 1)
                        e_scr[l, rows_of[b], 2 * j * BIN:(2 * j + 2) * BIN] = es[b]
                    for b in bins:
                        part = dot(es[b], jnp.concatenate([pair_rows(v[rows_of[b]], j), mask_pairs[j]], 1))
                        acc[b] = part if acc[b] is None else acc[b] + part
                for b in bins:
                    rl = 1.0 / acc[b][:, width:]
                    mixed_bins.append((acc[b][:, :width] * rl).astype(bf16))
                    rl_bins.append(rl)
            mixed = jnp.concatenate(mixed_bins, 0)
            rl = jnp.concatenate(rl_bins, 0)
            x1 = x + dot(mixed, wout[l]) + outb[l, 0:1, :]
            n2, rstd2 = norm_parts(x1)
            h2 = (n2 * gains[l, 1:2, :] + shifts[l, 1:2, :]).astype(bf16)
            hid = dot(jnp.concatenate([h2, ones_lanes], 1), half_up[l])
            sq = hid * hid
            t = 1.0 + jnp.tanh(hid * (2 * GELU_C + (8 * GELU_C * GELU_K) * sq))
            act = hid * t
            act_b = act.astype(bf16)
            act_scr[l] = act_b
            rest = (2.0 - t).astype(bf16)
            slope = jnp.asarray(2 * GELU_C, bf16) + jnp.asarray(24 * GELU_C * GELU_K, bf16) * sq.astype(bf16)
            gp_scr[l] = t.astype(bf16) + act_b * rest * slope
            saved.append((n1, rstd1, h1, q, k, v, mixed, rl, n2, rstd2, h2))
            x = x1 + dot(act_b, wdown[l]) + outb[l, 1:2, :]

        out_b = x.astype(bf16)
        for l in reversed(range(LAYERS)):
            n1, rstd1, h1, q, k, v, mixed, rl, n2, rstd2, h2 = saved[l]
            e2 = g.astype(bf16)
            a_small[l, 7:8, :] += row_sum(e2.astype(f32))
            du = dot_nt(e2, half_down[l]).astype(bf16) * gp_scr[l]
            dh2 = dot_nt(du, wup[l])
            a_down[l] += dot(e2.T, act_scr[l])
            both_up = dot(jnp.concatenate([h2.T, ones_rows], 0), du)
            a_up[l] += both_up[:width]
            dus = both_up[width:width + 1]
            for c in range(hidden // width):
                a_small[l, 8 + c:9 + c, :] += dus[:, c * width:(c + 1) * width]
            a_small[l, 1:2, :] += row_sum(dh2 * n2)
            a_small[l, 3:4, :] += row_sum(dh2)
            g1 = g + norm_back(dh2, n2, rstd2, gains[l, 1:2, :])
            e1 = g1.astype(bf16)
            dm = dot_nt(e1, wout[l])
            a_out[l] += dot(mixed.T, e1)
            a_small[l, 6:7, :] += row_sum(e1.astype(f32))
            dm1 = dm * rl
            dmo = -(dm1 * mixed.astype(f32))
            dm1 = dm1.astype(bf16)
            dmo = dmo.astype(bf16)
            rows_of = [slice(b * BIN, (b + 1) * BIN) for b in range(UNIT_BINS)]
            dqkv_bins = []
            for first in range(0, UNIT_BINS, BWD_GROUP):
                bins = range(first, first + BWD_GROUP)
                lhs = {b: jnp.concatenate([dm1[rows_of[b]], dmo[rows_of[b]]], 1) for b in bins}
                dm_t = {b: dm1[rows_of[b]].T for b in bins}
                q_t = {b: q[rows_of[b]].T for b in bins}
                v_t = {b: v[rows_of[b]].T for b in bins}
                dq = {b: None for b in bins}
                dv_t = {b: [] for b in bins}
                dk_t = {b: [] for b in bins}

                def d_scores(j):
                    return {b: dot(lhs[b], jnp.concatenate([pair_columns(v_t[b], j), mask_columns[j]], 0)) for b in bins}

                ahead = d_scores(0)
                for j in range(pairs):
                    top, low = 2 * j * HEAD, (2 * j + 2) * HEAD
                    z = ahead
                    if j + 1 < pairs:
                        ahead = d_scores(j + 1)
                    es = {b: e_scr[l, rows_of[b], 2 * j * BIN:(2 * j + 2) * BIN] for b in bins}
                    for b in bins:
                        pv = dot(dm_t[b][top:low], es[b])
                        dv_t[b] += [pv[:HEAD, :BIN], pv[HEAD:, BIN:]]
                    ds = {b: es[b] * z[b].astype(bf16) for b in bins}
                    for b in bins:
                        part = dot(ds[b], pair_rows(k[rows_of[b]], j))
                        dq[b] = part if dq[b] is None else dq[b] + part
                    for b in bins:
                        pk = dot(q_t[b][top:low], ds[b])
                        dk_t[b] += [pk[:HEAD, :BIN], pk[HEAD:, BIN:]]
                for b in bins:
                    dv = jnp.concatenate(dv_t[b], 0).T
                    dk = jnp.concatenate(dk_t[b], 0).T * LN2
                    dqkv_bins.append(jnp.concatenate([(dq[b] * HEAD ** -0.5).astype(bf16), dk.astype(bf16), dv.astype(bf16)], 1))
            dqkv = jnp.concatenate(dqkv_bins, 0)
            dh = dot_nt(dqkv, wqkv[l])
            both_qkv = dot(jnp.concatenate([h1.T, ones_rows], 0), dqkv)
            a_qkv[l] += both_qkv[:width]
            sums = both_qkv[width:width + 1]
            a_small[l, 4:5, :] += sums[:, :width]
            a_small[l, 5:6, :] += sums[:, 2 * width:]
            a_small[l, 0:1, :] += row_sum(dh * n1)
            a_small[l, 2:3, :] += row_sum(dh)
            g = g1 + norm_back(dh, n1, rstd1, gains[l, 0:1, :])

        grad_b = (g * factor).astype(bf16)
        s_iota = lax.broadcasted_iota(jnp.int32, (slot_rows, BIN), 0)
        p_iota = lax.broadcasted_iota(jnp.int32, (slot_rows, BIN), 1)
        both = jnp.concatenate([out_b, grad_b], 1)
        for b in range(UNIT_BINS):
            homes, picks = [], []
            for m in range(MEMBERS):
                slot = (u * UNIT_BINS + b) * MEMBERS + m
                t, o, n = mem_traj[slot], mem_off[slot], mem_len[slot]
                picks.append(jnp.where((p_iota - o == s_iota) & (s_iota < n), 1.0, 0.0).astype(bf16))
                homes.append(jnp.where(n > 0, t, trajs))
            rows = dot(jnp.concatenate(picks, 0), both[b * BIN:(b + 1) * BIN]).astype(bf16)
            for m, home in enumerate(homes):
                out[home] = rows[m * slot_rows:(m + 1) * slot_rows, :width]
                gtok[home] = rows[m * slot_rows:(m + 1) * slot_rows, width:]
        return carry

    lax.fori_loop(0, units, body, 0)

    stores = [
        pltpu.make_async_copy(out.at[pl.ds(0, trajs)], out_hbm, sems.at[0]),
        pltpu.make_async_copy(gtok.at[pl.ds(0, trajs)], gtok_hbm, sems.at[1]),
    ]
    for copy in stores:
        copy.start()
    for l in range(LAYERS):
        at = 0
        for c in range(3):
            gsum[l, at:at + width, :] = a_qkv[l, :, c * width:(c + 1) * width].astype(bf16)
            at += width
        gsum[l, at:at + width, :] = a_out[l].astype(bf16)
        at += width
        for c in range(hidden // width):
            gsum[l, at:at + width, :] = a_up[l, :, c * width:(c + 1) * width].astype(bf16)
            at += width
        for c in range(hidden // width):
            gsum[l, at:at + width, :] = a_down[l, :, c * width:(c + 1) * width].T.astype(bf16)
            at += width
        gsum[l, at:at + SMALL, :] = a_small[l].astype(bf16)
    mine = parity[0]
    half = gsum.shape[1] // 2
    stores += [
        pltpu.make_async_copy(gsum.at[l, pl.ds(i * half, half)], to, sems.at[2 + 2 * k + i])
        for k, (l, pair) in enumerate(((1 - mine, (other_a, other_b)), (mine, (mine_a, mine_b))))
        for i, to in enumerate(pair)
    ]
    for copy in stores[2:]:
        copy.start()
    for copy in stores:
        copy.wait()


def main_call(args, steps_top, parity):
    tokens, lengths, gains, shifts, wqkv, qvb, wout, outb, wup, upb, wdown, cot = args
    trajs, slot_rows, width = tokens.shape
    hidden = wup.shape[2]
    unit = BIN * UNIT_BINS
    slots = 2 * (trajs + UNIT_BINS)
    per_layer = 4 * width + 2 * hidden + SMALL
    sm = pl.BlockSpec(memory_space=pltpu.SMEM)
    hbm = pl.BlockSpec(memory_space=pl.ANY)
    sums = jax.ShapeDtypeStruct((per_layer // 2, width), bf16)
    return pl.pallas_call(
        functools.partial(main_kernel, steps_top=steps_top),
        out_shape=(
            jax.ShapeDtypeStruct(tokens.shape, bf16),
            jax.ShapeDtypeStruct(tokens.shape, bf16),
            sums,
            sums,
            sums,
            sums,
        ),
        in_specs=[sm, sm] + [hbm] * 11,
        out_specs=(hbm,) * 6,
        scratch_shapes=[
            pltpu.VMEM(tokens.shape, bf16),
            pltpu.VMEM(tokens.shape, bf16),
        ]
        + [pltpu.VMEM(a.shape, a.dtype) for a in (gains, shifts, wqkv, qvb, wout, outb, wup, upb, wdown)]
        + [
            pltpu.VMEM((trajs + 1, slot_rows, width), bf16),
            pltpu.VMEM((trajs + 1, slot_rows, width), bf16),
            pltpu.VMEM((LAYERS, per_layer, width), bf16),
            pltpu.VMEM((LAYERS, width, 3 * width), f32),
            pltpu.VMEM((LAYERS, width, width), f32),
            pltpu.VMEM((LAYERS, width, hidden), f32),
            pltpu.VMEM((LAYERS, width, hidden), f32),
            pltpu.VMEM((LAYERS, SMALL, width), f32),
            pltpu.VMEM((LAYERS, unit, width // HEAD * BIN), bf16),
            pltpu.VMEM((LAYERS, unit, hidden), bf16),
            pltpu.VMEM((LAYERS, unit, hidden), bf16),
            pltpu.VMEM((LAYERS, 2 * width, hidden), bf16),
            pltpu.VMEM((LAYERS, hidden, width), bf16),
            pltpu.SMEM((trajs,), jnp.int32),
            pltpu.SMEM((steps_top + 1,), jnp.int32),
            pltpu.SMEM((slots,), jnp.int32),
            pltpu.SMEM((slots,), jnp.int32),
            pltpu.SMEM((slots,), jnp.int32),
            pltpu.SemaphoreType.DMA((11,)),
        ],
        compiler_params=pltpu.CompilerParams(vmem_limit_bytes=56 * 1024 * 1024),
        name="layers",
    )(lengths, parity, tokens, cot, gains, shifts, wqkv, qvb, wout, outb, wup, upb, wdown)


AXES = ("dp", "group")


def finish_kernel(parity, mine_a, mine_b, other_a, other_b, gains, shifts, qkv, qvb, out, outb, up, upb, down):
    rows, width = mine_a.shape
    hidden = up.shape[2]
    for p in range(LAYERS):

        @pl.when(parity[0] == p)
        def _():
            for l in range(LAYERS):
                pieces = (mine_a, mine_b) if l == p else (other_a, other_b)

                def take(at, count):
                    found = []
                    while count > 0:
                        piece, first = divmod(at, rows)
                        now = min(count, rows - first)
                        found.append(pieces[piece][first:first + now, :].astype(f32))
                        at, count = at + now, count - now
                    return found[0] if len(found) == 1 else jnp.concatenate(found, 0)

                at = 0
                for c in range(3):
                    qkv[l, :, c * width:(c + 1) * width] = take(at, width)
                    at += width
                out[l] = take(at, width)
                at += width
                for c in range(hidden // width):
                    up[l, :, c * width:(c + 1) * width] = take(at, width)
                    at += width
                down[l] = take(at, hidden)
                at += hidden
                small = take(at, SMALL)
                gains[l] = small[0:2]
                shifts[l] = small[2:4]
                qvb[l] = small[4:6]
                outb[l] = small[6:8]
                for c in range(hidden // width):
                    upb[l:l + 1, c * width:(c + 1) * width] = small[8 + c:9 + c]


def finish_call(parity, mine, other, args):
    vm = pl.BlockSpec(memory_space=pltpu.VMEM)
    sm = pl.BlockSpec(memory_space=pltpu.SMEM)
    return pl.pallas_call(
        finish_kernel,
        out_shape=tuple(jax.ShapeDtypeStruct(a.shape, f32) for a in args[2:11]),
        in_specs=[sm] + [vm] * 4,
        out_specs=(vm,) * 9,
        compiler_params=pltpu.CompilerParams(vmem_limit_bytes=16 * 1024 * 1024),
        name="finish",
    )(parity, *mine, *other)


def exchange(x, bits, devices):
    return lax.ppermute(x, AXES, [(i, i ^ bits[i % 2]) for i in range(devices)])


def added(a, b):
    return (a.astype(f32) + b.astype(f32)).astype(bf16)


def picked(pieces, at):
    first, low = (at // 2) % 2 == 0, at % 2 == 0
    return jnp.where(first, jnp.where(low, pieces[0], pieces[1]), jnp.where(low, pieces[2], pieces[3]))


def all_sum(mine, other, index, devices):
    parts = [added(m, exchange(o, (1, 1), devices)) for m, o in zip(mine, other)]
    half = parts[0].shape[0] // 2
    quarters = [parts[0][:half], parts[0][half:], parts[1][:half], parts[1][half:]]
    bits = [1 << i for i in range(1, devices.bit_length() - 1)]
    rest = bits[2:]
    crossed = list(rest)
    for i in range(0, len(rest) - 1, 2):
        crossed[i], crossed[i + 1] = rest[i + 1], rest[i]
    turns = {m: m * bits[0] for m in (1, 2, 3)}
    place = (index // bits[0]) % 4
    got = [exchange(picked(quarters, place ^ m), (bit, bit), devices) for m, bit in turns.items()]
    total = picked(quarters, place).astype(f32)
    for piece in got:
        total = total + piece.astype(f32)
    total = total.astype(bf16)
    for step in zip(rest, crossed):
        total = added(total, exchange(total, step, devices))
    have = {0: total}
    for m, bit in turns.items():
        have[m] = exchange(total, (bit, bit), devices)
    pieces = [have[m] for m in range(4)]
    parts = [jnp.concatenate([picked(pieces, place ^ j), picked(pieces, place ^ (j + 1))]) for j in (0, 2)]
    return parts, [exchange(p, (1, 1), devices) for p in parts]


def solution(mesh):
    mesh_shape = dict(mesh.shape)
    devices = mesh_shape["dp"] * mesh_shape["group"]

    def per_device(*args):
        index = lax.axis_index("dp") * mesh_shape["group"] + lax.axis_index("group")
        parity = (index % 2).astype(jnp.int32).reshape(1)
        output, grad_tokens, mine_a, mine_b, other_a, other_b = main_call(args, STEPS, parity)
        mine, other = all_sum((mine_a, mine_b), (other_a, other_b), index, devices)
        return (output, grad_tokens) + tuple(finish_call(parity, mine, other, args))

    rows = P(AXES, None, None)
    return jax.shard_map(
        per_device,
        mesh=mesh,
        in_specs=(rows, P(AXES)) + (P(),) * 9 + (rows,),
        out_specs=(rows, rows) + (P(),) * 9,
        check_vma=False,
    )
```
